128 devices in a mesh: tm: 32 (over y, z, core), mp: 4 (over x).
Axes of the slice: x: 4, y: 4, z: 4, core: 2. Of those that a mesh axis runs over, the one named last changes fastest.
Arguments:
- tokens: bfloat16 [32768, 2048], P('tm'), may hold values from -6 to 6
- gain_self: bfloat16 [2048], replicated, may hold values from 0.099609375 to 1.8984375
- gain_cross: bfloat16 [2048], replicated, may hold values from 0.099609375 to 1.8984375
- w_query: bfloat16 [2048, 2048], P(None, 'mp'), may hold values from -0.6629126 to 0.6629126
- w_key: bfloat16 [2048, 2048], P(None, 'mp'), may hold values from -0.6629126 to 0.6629126
- w_value: bfloat16 [2048, 2048], P(None, 'mp'), may hold values from -0.125 to 0.125
- w_out: bfloat16 [2048, 2048], P('mp'), may hold values from -0.125 to 0.125
- w_cross_query: bfloat16 [2048, 2048], P(None, 'mp'), may hold values from -0.6629126 to 0.6629126
- w_cross_out: bfloat16 [2048, 2048], P('mp'), may hold values from -0.125 to 0.125
- w_text_key: bfloat16 [1024, 2048], P(None, 'mp'), may hold values from -0.9375 to 0.9375
- w_text_value: bfloat16 [1024, 2048], P(None, 'mp'), may hold values from -0.1875 to 0.1875
- text_states: bfloat16 [64, 512, 1024], P('tm'), may hold values from -6 to 6
- song_of_block: int32 [64], replicated, may hold values from 0 to 31, never falling along the last dimension, each value on 1 to 4 neighbouring positions
- last_fill: int32 [32], replicated, may hold values from 1 to 512
Outputs:
- mixed: bfloat16 [32768, 2048], P('tm', 'mp')
The draws below stay inside these ranges and needn't reach their ends.
Inputs may be any that keep to these rules, and one draw needn't show every extreme that they name: `song_of_block`: song ids never fall along the blocks; each song covers 1 to 4 consecutive blocks, one exactly 4.
All inputs are finite; a program needn't handle non-finite values.
Results may differ from the reference program's by a relative error of at most 0.025.
Values may be sent and summed in bfloat16 or wider, within the bound.
A program may use at most 192 MiB of HBM per device.

```python
import math
import jax
import jax.numpy as jnp
import numpy as np
from jax import lax

D = 2048
HEADS = 32
HD = 64
TD = 1024
TXT = 512
BLK = 512
MAXB = 4
BLOCKS = 64
SONGS = 32
TOKENS = 32768
N_MP = 4


def head_strengths(key, salt):
    key = jax.random.fold_in(key, salt)
    order = jax.random.permutation(key, HEADS)
    rank = jnp.argsort(order).astype(jnp.int32)
    frac = rank.astype(jnp.float32) / max(HEADS - 1, 1)
    strength = 0.8 * jnp.power(2.25, frac)
    return jnp.repeat(strength, HD).astype(jnp.float32)


def draw_w_query(key, part):
    strengths = head_strengths(key, 11)
    key = jax.random.fold_in(key, 1)
    base = jnp.clip(jax.random.normal(key, (D, HEADS * HD), jnp.float32), -4.0, 4.0)
    return (base * D ** (-0.5) * strengths[None, :]).astype(jnp.bfloat16)


def draw_w_key(key, part):
    strengths = head_strengths(key, 11)
    key = jax.random.fold_in(key, 2)
    base = jnp.clip(jax.random.normal(key, (D, HEADS * HD), jnp.float32), -4.0, 4.0)
    return (base * D ** (-0.5) * strengths[None, :]).astype(jnp.bfloat16)


def draw_w_cross_query(key, part):
    strengths = head_strengths(key, 23)
    key = jax.random.fold_in(key, 3)
    base = jnp.clip(jax.random.normal(key, (D, HEADS * HD), jnp.float32), -4.0, 4.0)
    return (base * D ** (-0.5) * strengths[None, :]).astype(jnp.bfloat16)


def draw_w_text_key(key, part):
    strengths = head_strengths(key, 23)
    key = jax.random.fold_in(key, 4)
    base = jnp.clip(jax.random.normal(key, (TD, HEADS * HD), jnp.float32), -4.0, 4.0)
    return (base * TD ** (-0.5) * strengths[None, :]).astype(jnp.bfloat16)


def touch_ends(entries, stream_key, least, top_value):
    longest = entries.shape.index(max(entries.shape))
    spots = []
    for shift in (0, 1):
        where = [jax.random.randint(jax.random.fold_in(stream_key, axis), (), 0, length) for axis, length in enumerate(entries.shape)]
        where[longest] = (where[longest] + shift) % entries.shape[longest]
        spots.append(tuple(where))
    return entries.at[spots[0]].set(least).at[spots[1]].set(top_value)


def block_levels(own_key, dims, shards, low, largest):
    level = 1.0
    for axis_at, blocks in shards:
        draws = jax.random.uniform(jax.random.fold_in(jax.random.fold_in(own_key, 6), axis_at), (blocks,), jnp.float32, low / len(shards), largest / len(shards))
        level = level * jnp.repeat(jnp.exp(draws), dims[axis_at] // blocks).reshape((-1,) + (1,) * (len(dims) - 1 - axis_at))
    return level


def length_profile(count, total, reach, lean):
    weights = [(1 << 20) // math.isqrt(grade ** lean) + 1 for grade in range(2, count + 1)]
    spare, counts = total - reach - (count - 1), [1] * (count - 1)
    while spare > 0:
        candidates = [i for i in range(count - 1) if counts[i] < reach]
        pool, budget = sum([weights[i] for i in candidates]), spare
        for i in candidates:
            extra = min(reach - counts[i], max(1, budget * weights[i] // pool), spare)
            counts[i] = counts[i] + extra
            spare = spare - extra
    return np.array([reach] + counts)


def ragged(own_key, number_of, total, most, slope):
    if number_of == 2:
        one = jax.random.randint(own_key, (), max(1, total - most), min(most, total - 1) + 1)
        return jnp.stack([one, total - one])
    lengths = jnp.asarray(length_profile(number_of, total, most, slope), jnp.int32)
    pairs = (number_of - 1) // 2
    giver, taker = lengths[1:1 + 2 * pairs:2], lengths[2:2 + 2 * pairs:2]
    slack = jnp.minimum(giver - 1, most - taker)
    moved = jax.random.randint(jax.random.fold_in(own_key, 1), (pairs,), 0, 1 << 20) % (slack + 1)
    lengths = lengths.at[1:1 + 2 * pairs:2].set(giver - moved).at[2:2 + 2 * pairs:2].set(taker + moved)
    return lengths[jax.random.permutation(jax.random.fold_in(own_key, 2), number_of)]


def noise(own_key, shape, spread, bound, shards=(), kind=jnp.bfloat16):
    factor_of = block_levels(own_key, shape, shards, -0.22, 0.18) if shards else 1.0
    values = jax.random.normal(own_key, shape, jnp.float32) * spread * factor_of
    return jnp.minimum(jnp.maximum(values, -bound), bound).astype(kind)


def setup_inputs(seed: int = 0) -> dict:
    key_list = jax.random.split(jax.random.key(seed), 15)
    tokens = noise(key_list[0], (TOKENS, D), 1.0, 6.0, ((0, 32),))
    gain_self = jnp.clip(1.0 + 0.18 * jax.random.normal(key_list[1], (D,), jnp.float32), 0.099609375, 1.8984375).astype(jnp.bfloat16)
    gain_cross = jnp.clip(1.0 + 0.18 * jax.random.normal(key_list[2], (D,), jnp.float32), 0.099609375, 1.8984375).astype(jnp.bfloat16)
    w_query = draw_w_query(jax.random.fold_in(key_list[14], 71), 0)
    w_key = draw_w_key(jax.random.fold_in(key_list[14], 71), 0)
    w_value = noise(key_list[5], (D, HEADS * HD), D ** -0.5, 0.125, ((1, 4),))
    w_out = noise(key_list[6], (HEADS * HD, D), (HEADS * HD) ** -0.5, 0.125, ((0, 4),))
    w_cross_query = draw_w_cross_query(jax.random.fold_in(key_list[14], 71), 0)
    w_cross_out = noise(key_list[8], (HEADS * HD, D), (HEADS * HD) ** -0.5, 0.125, ((0, 4),))
    w_text_key = draw_w_text_key(jax.random.fold_in(key_list[14], 71), 0)
    w_text_value = noise(key_list[10], (TD, HEADS * HD), TD ** -0.5, 0.1875, ((1, 4),))
    text_states = noise(key_list[11], (BLOCKS, TXT, TD), 1.0, 6.0, ((0, 32),))
    song_of_block = jnp.searchsorted(jnp.cumsum(ragged(key_list[12], SONGS, BLOCKS, MAXB, 2)), jnp.arange(BLOCKS), side="right").astype(jnp.int32)
    last_fill = touch_ends(jax.random.randint(key_list[13], (SONGS,), 1, BLK + 1), jax.random.fold_in(key_list[13], 1), 1, BLK).astype(jnp.int32)
    return {"tokens": tokens, "gain_self": gain_self, "gain_cross": gain_cross, "w_query": w_query, "w_key": w_key, "w_value": w_value, "w_out": w_out, "w_cross_query": w_cross_query, "w_cross_out": w_cross_out, "w_text_key": w_text_key, "w_text_value": w_text_value, "text_states": text_states, "song_of_block": song_of_block, "last_fill": last_fill}


epsilon = 1e-05

def normalize(values, gain):
    meansq = lax.optimization_barrier(jnp.mean(values * values, axis=-1, keepdims=True))
    return values * lax.rsqrt(meansq + epsilon) * gain.astype(jnp.float32)

def attend(query, keys, value_rows, allowed, head_dim):
    heads = query.shape[1] // head_dim
    query_heads = query.reshape(query.shape[0], heads, head_dim).astype(jnp.float32)
    key_heads = keys.reshape(keys.shape[0], heads, head_dim).astype(jnp.float32)
    value_heads = value_rows.reshape(value_rows.shape[0], heads, head_dim).astype(jnp.float32)
    scores = jnp.einsum('qhd,khd->hqk', query_heads, key_heads) * head_dim ** (-0.5)
    if allowed is not None:
        scores = jnp.where(allowed[None], scores, -1e+30)
    top = lax.optimization_barrier(jnp.max(scores, axis=-1, keepdims=True))
    weights = jnp.exp(scores - top)
    probs = (weights / lax.optimization_barrier(jnp.sum(weights, axis=-1, keepdims=True))).astype(jnp.bfloat16)
    mixed = jnp.einsum('hqk,khd->qhd', probs.astype(jnp.float32), value_heads)
    return mixed.reshape(query.shape[0], heads * head_dim).astype(jnp.bfloat16)

def group_sum(context, weight):
    share = context.shape[1] // N_MP
    total = jnp.zeros((context.shape[0], weight.shape[1]), jnp.float32)
    for group in range(N_MP):
        term = jnp.dot(context[:, group * share:(group + 1) * share], weight[group * share:(group + 1) * share], preferred_element_type=jnp.float32)
        total = total + lax.optimization_barrier(term.astype(jnp.bfloat16)).astype(jnp.float32)
    return total

def reference(tokens, gain_self, gain_cross, w_query, w_key, w_value, w_out, w_cross_query, w_cross_out, w_text_key, w_text_value, text_states, song_of_block, last_fill):
    cols = w_query.shape[1]
    blocks = song_of_block.shape[0]
    normed = normalize(tokens.astype(jnp.float32), gain_self).astype(jnp.bfloat16)
    query = jnp.dot(normed, w_query, preferred_element_type=jnp.float32).astype(jnp.bfloat16)
    keys = jnp.dot(normed, w_key, preferred_element_type=jnp.float32).astype(jnp.bfloat16)
    value_rows = jnp.dot(normed, w_value, preferred_element_type=jnp.float32).astype(jnp.bfloat16)
    block_ids = jnp.arange(blocks, dtype=jnp.int32)
    is_last = jnp.concatenate([song_of_block[1:] != song_of_block[:-1], jnp.ones((1,), bool)])
    filled = jnp.where(is_last, last_fill[song_of_block], BLK).astype(jnp.int32)
    before = jnp.concatenate([jnp.full((1,), -1, jnp.int32), song_of_block[:-1]])
    starts = song_of_block != before
    first = lax.cummax(jnp.where(starts, block_ids, 0).astype(jnp.int32), axis=0)
    padding = jnp.zeros((BLK, cols), jnp.bfloat16)
    keys_ext = jnp.concatenate([padding, keys])
    values_ext = jnp.concatenate([padding, value_rows])
    position = jnp.arange(BLK, dtype=jnp.int32)

    def self_block(index):
        rows_q = lax.dynamic_slice_in_dim(query, index * BLK, BLK)
        window_keys = lax.dynamic_slice_in_dim(keys_ext, index * BLK, 2 * BLK)
        window_values = lax.dynamic_slice_in_dim(values_ext, index * BLK, 2 * BLK)
        same = before[index] == song_of_block[index]
        allowed_prev = same & (position[None, :] > position[:, None])
        allowed_own = (position[None, :] <= position[:, None]) & (position[None, :] < filled[index])
        allowed = jnp.concatenate([allowed_prev, allowed_own], axis=1)
        return attend(rows_q, window_keys, window_values, allowed, HD)
    context = lax.map(self_block, block_ids).reshape(TOKENS, cols)
    hidden = tokens.astype(jnp.float32) + group_sum(context, w_out)
    normed_cross = normalize(hidden, gain_cross).astype(jnp.bfloat16)
    cross_query = jnp.dot(normed_cross, w_cross_query, preferred_element_type=jnp.float32).astype(jnp.bfloat16)

    def cross_block(index):
        text = text_states[first[index]]
        text_keys = jnp.dot(text, w_text_key, preferred_element_type=jnp.float32).astype(jnp.bfloat16)
        text_values = jnp.dot(text, w_text_value, preferred_element_type=jnp.float32).astype(jnp.bfloat16)
        rows_q = lax.dynamic_slice_in_dim(cross_query, index * BLK, BLK)
        return attend(rows_q, text_keys, text_values, None, HD)
    cross_context = lax.map(cross_block, block_ids).reshape(TOKENS, cols)
    return (hidden + group_sum(cross_context, w_cross_out)).astype(jnp.bfloat16)
```

```python
import jax
import jax.numpy as jnp
from jax import lax
from jax.experimental import pallas as pl
from jax.experimental.pallas import tpu as pltpu
from jax.sharding import PartitionSpec as P

F32 = jnp.float32
BF16 = jnp.bfloat16
EPS = 1e-05
MESH = pl.DeviceIdType.MESH
BLK = 512
TILE = 256
COLS = 512
WIDTH = 2048
CHUNKS = ((1, 0), (1, 1), (0, 0), (0, 1))
REMOTE = 80


def dot(a, b):
    return jnp.dot(a, b, preferred_element_type=F32)


def dot_t(a, b):
    return lax.dot_general(a, b, (((1,), (1,)), ((), ())), preferred_element_type=F32)


def kernel(
    tokens, gain_s, gain_c, w_q, w_k, w_v, w_o, w_cq, w_co, w_tk, w_tv, text, song, fill,
    out,
    tok, nrm, wq, wk, wv, wo, wcq, wco, wtk, wtv, txt, tin, ta, tb,
    q, k, v, kp, vp, ctx, hid, acc, part, rs1, rs2, fwd, tk, tv, bias, cc, ob,
    lsem, ssem, rsem,
):
    t, x = lax.axis_index("tm"), lax.axis_index("mp")
    core, y = lax.rem(t, 2), t // 8
    right, left, across = lax.rem(x + 1, 4), lax.rem(x + 3, 4), lax.rem(x + 2, 4)
    to_right, to_left = {"mp": right}, {"mp": left}
    up, down = {"tm": lax.rem(t + 8, 32)}, {"tm": lax.rem(t + 24, 32)}
    next1, next2 = {"tm": lax.rem(t + 1, 32)}, {"tm": lax.rem(t + 2, 32)}
    prev1, prev2 = {"tm": lax.rem(t + 31, 32)}, {"tm": lax.rem(t + 30, 32)}
    sibling = {"tm": t + 1 - 2 * core}

    loads = {}

    def load(name, src, dst):
        copy = pltpu.make_async_copy(src, dst, lsem.at[len(loads)])
        copy.start()
        loads[name] = copy

    def loaded(*names):
        for name in names:
            loads[name].wait()

    barrier = pltpu.get_barrier_semaphore()
    for peer in (prev1, prev2, to_right, to_left, up, down, sibling):
        pl.semaphore_signal(barrier, inc=1, device_id=peer, device_id_type=MESH)
    load("tok1", tokens.at[pl.ds(BLK, BLK)], tok.at[pl.ds(BLK, BLK)])
    load("wk", w_k, wk)
    load("wv", w_v, wv)
    load("tok0", tokens.at[pl.ds(0, BLK)], tok.at[pl.ds(0, BLK)])
    load("wq", w_q, wq)
    load("text", text, txt)
    load("wo", w_o, wo.at[x])
    load("wtk", w_tk, wtk)
    load("wtv", w_tv, wtv)
    load("wcq", w_cq, wcq)
    load("wco", w_co, wco)

    sent = []
    count = [0]

    def fresh():
        count[0] += 1
        return count[0] - 1

    def remote(src, dst, to, n):
        return pltpu.make_async_remote_copy(
            src_ref=src, dst_ref=dst, send_sem=ssem.at[n], recv_sem=rsem.at[n],
            device_id=to, device_id_type=MESH,
        )

    def send(src, dst, to, n):
        copy = remote(src, dst, to, n)
        copy.start()
        sent.append(copy)

    def landed(ref, n):
        remote(ref, ref, to_right, n).wait_recv()

    class Gather:
        def __init__(self, me, after, before, src, at):
            self.me, self.after, self.before, self.src, self.at = me, after, before, src, at
            self.n = [fresh() for _ in range(4)]

        def start(self):
            send(self.src, self.at(self.me, None), self.after, self.n[0])
            send(self.src, self.at(self.me, None), self.before, self.n[1])

        def forward(self):
            lo, hi = lax.rem(self.me + 3, 4), lax.rem(self.me + 1, 4)
            landed(self.at(lo, None), self.n[0])
            send(self.at(lo, 0), self.at(lo, 0), self.after, self.n[2])
            landed(self.at(hi, None), self.n[1])
            send(self.at(hi, 1), self.at(hi, 1), self.before, self.n[3])

        def finish(self):
            far = lax.rem(self.me + 2, 4)
            landed(self.at(far, 0), self.n[2])
            landed(self.at(far, 1), self.n[3])

    def halves(ref, half, size):
        return ref if half is None else ref.at[pl.ds(half * size, size)]

    others = [lax.rem(x + d, 4) for d in (1, 3, 2)]
    wo_x = Gather(
        x, to_right, to_left, w_o.at[core, y], lambda i, h: halves(wo.at[i, core, y], h, 32)
    )
    wo_y = [
        Gather(
            y, up, down, wo.at[g, core, y], lambda i, h, g=g: halves(wo.at[g, core, i], h, 32)
        )
        for g in others
    ]
    wo_n = [fresh() for _ in others]
    text_n = [fresh() for _ in range(3)]
    text_x = Gather(x, to_right, to_left, tin.at[x], lambda i, h: halves(tin.at[i], h, 64))
    kv_n = [fresh() for _ in range(2)]

    pl.semaphore_wait(barrier, 7)
    send(text.at[0, x], ta.at[0], next1, text_n[0])
    send(text.at[1, x], ta.at[1], next1, text_n[1])
    send(text.at[1, x], tb, next2, text_n[2])
    wo_x.start()

    b0 = 2 * t
    s0, s1 = song[b0], song[b0 + 1]
    m1 = song[jnp.maximum(b0 - 1, 0)]
    m2 = song[jnp.maximum(b0 - 2, 0)]
    m3 = song[jnp.maximum(b0 - 3, 0)]
    p2 = song[jnp.minimum(b0 + 2, 63)]
    same = [(t > 0) & (m1 == s0), s0 == s1]
    filled = [
        jnp.where(s0 != s1, fill[s0], BLK),
        jnp.where((t == 31) | (p2 != s1), fill[s1], BLK),
    ]
    second_starts = m1 != m2
    first_starts = (t == 1) | (m2 != m3)

    def normed(block):
        gain = gain_s[...].astype(F32)

        @pl.loop(0, BLK // 32)
        def _(i):
            values = tok[pl.ds(pl.multiple_of(block * BLK + i * 32, 32), 32), :].astype(F32)
            meansq = jnp.mean(values * values, axis=-1, keepdims=True)
            nrm[pl.ds(pl.multiple_of(i * 32, 32), 32), :] = (
                values * lax.rsqrt(meansq + EPS) * gain
            ).astype(BF16)

    def project(a, w, dst, row, scale=None):
        @pl.loop(0, COLS // 256)
        def _(i):
            cols = pl.ds(pl.multiple_of(i * 256, 256), 256)
            res = dot(a[...], w[:, cols]).astype(BF16)
            if scale is not None:
                res = res * jnp.asarray(scale, BF16)
            dst[pl.ds(row, a.shape[0]), cols] = res

    loaded("tok1")
    normed(1)
    loaded("wk")
    project(nrm, wk, k, BLK)
    send(k.at[pl.ds(BLK, BLK)], kp, next1, kv_n[0])
    loaded("wv")
    project(nrm, wv, v, BLK)
    send(v.at[pl.ds(BLK, BLK)], vp, next1, kv_n[1])
    wo_x.forward()
    loaded("wq")
    project(nrm, wq, q, BLK, 0.125)
    landed(ta.at[0], text_n[0])
    landed(ta.at[1], text_n[1])
    landed(tb, text_n[2])
    tin[x] = jnp.where(second_starts, ta[1], jnp.where(first_starts, ta[0], tb[...]))
    text_x.start()
    wo_x.finish()
    for gather in wo_y:
        gather.start()
    loaded("tok0")
    normed(0)
    project(nrm, wk, k, 0)
    project(nrm, wv, v, 0)
    project(nrm, wq, q, 0, 0.125)
    text_x.forward()

    lane = lax.broadcasted_iota(jnp.int32, (1, 128), 1)
    pick = [(lane < 64).astype(F32).astype(BF16), (lane >= 64).astype(F32).astype(BF16)]
    ones = jnp.ones((TILE, 128), BF16)

    def softmax_parts(tiles):
        top = tiles[0].max(axis=-1, keepdims=True)
        for s in tiles[1:]:
            top = jnp.maximum(top, s.max(axis=-1, keepdims=True))
        return [jnp.exp(s - top) for s in tiles]

    def with_ones(rows):
        return jnp.concatenate([rows, ones], axis=1)

    def ratio(mixed):
        return mixed[:, :128] / mixed[:, 128:]

    def self_chunk(block, half):
        row = block * BLK + half * TILE
        before_k, before_v = (k, v) if block == 1 else (kp, vp)
        i = lax.broadcasted_iota(jnp.int32, (TILE, BLK), 0) + half * TILE
        j = lax.broadcasted_iota(jnp.int32, (TILE, BLK), 1)
        limit = jnp.where(j <= i, filled[block], jnp.where(same[block], BLK, 0))
        bias[...] = jnp.where(j < limit, 0.0, -1e30)
        lower = lax.broadcasted_iota(jnp.int32, (TILE, TILE), 1) <= lax.broadcasted_iota(
            jnp.int32, (TILE, TILE), 0
        )

        @pl.loop(0, COLS // 128)
        def _(pair):
            cols = pl.ds(pl.multiple_of(pair * 128, 128), 128)
            queries = q[pl.ds(row, TILE), cols]
            halves_out = []
            for head in range(2):
                query = queries * pick[head]
                scores = []
                for tile in range(2):
                    own = pl.ds(block * BLK + tile * TILE, TILE)
                    earlier = pl.ds(tile * TILE, TILE)
                    if tile < half:
                        s = dot_t(query, k[own, cols])
                    elif tile > half:
                        s = dot_t(query, before_k[earlier, cols])
                    else:
                        s = jnp.where(
                            lower,
                            dot_t(query, k[own, cols]),
                            dot_t(query, before_k[earlier, cols]),
                        )
                    scores.append(s + bias[:, tile * TILE : (tile + 1) * TILE])
                weights = softmax_parts(scores)
                mixed = None
                for tile in range(2):
                    own = pl.ds(block * BLK + tile * TILE, TILE)
                    earlier = pl.ds(tile * TILE, TILE)
                    w = weights[tile]
                    if tile < half:
                        terms = [(w, v[own, cols])]
                    elif tile > half:
                        terms = [(w, before_v[earlier, cols])]
                    else:
                        terms = [
                            (jnp.where(lower, w, 0.0), v[own, cols]),
                            (jnp.where(lower, 0.0, w), before_v[earlier, cols]),
                        ]
                    for a, b in terms:
                        term = dot(a.astype(BF16), with_ones(b))
                        mixed = term if mixed is None else mixed + term
                halves_out.append(ratio(mixed))
            ctx[x, pl.ds(row, TILE), cols] = jnp.where(lane < 64, *halves_out).astype(BF16)

    ctx_x = [
        Gather(
            x, to_right, to_left, ctx.at[x, pl.ds(b * BLK + h * TILE, TILE)],
            lambda i, part, r=b * BLK + h * TILE: (
                ctx.at[i, pl.ds(r, TILE)]
                if part is None
                else ctx.at[i, pl.ds(r + part * TILE // 2, TILE // 2)]
            ),
        )
        for b, h in CHUNKS
    ]

    self_chunk(*CHUNKS[0])
    ctx_x[0].start()
    for gather in wo_y:
        gather.forward()
    self_chunk(*CHUNKS[1])
    ctx_x[1].start()
    ctx_x[0].forward()
    for gather, g, n in zip(wo_y, others, wo_n):
        gather.finish()
        send(wo.at[g, core], wo.at[g, core], sibling, n)
    landed(kp, kv_n[0])
    landed(vp, kv_n[1])
    self_chunk(*CHUNKS[2])
    ctx_x[2].start()
    ctx_x[1].forward()
    self_chunk(*CHUNKS[3])
    ctx_x[3].start()
    ctx_x[2].forward()

    text_x.finish()
    loaded("text", "wtk", "wtv")

    @pl.loop(0, 4)
    def _(i):
        first = jnp.where(same[0], tin[i], txt[0, i])
        txt[0, i] = first
        txt[1, i] = jnp.where(same[1], first, txt[1, i])

    for block in (1, 0):
        source = txt[block].reshape(BLK, 1024)

        for w, dst in ((wtk, tk), (wtv, tv)):
            @pl.loop(0, COLS // 256)
            def _(i, w=w, dst=dst, source=source, block=block):
                cols = pl.ds(pl.multiple_of(i * 256, 256), 256)
                rows = txt[block].reshape(BLK, 1024)
                dst[block, :, cols] = dot(rows, w[:, cols]).astype(BF16)
    ctx_x[3].forward()

    rs_n = [[fresh() for _ in range(6)] for _ in CHUNKS]
    low, high = pl.ds(0, TILE // 2), pl.ds(TILE // 2, TILE // 2)

    def cross_chunk(c, block, half):
        row = block * BLK + half * TILE
        rows = pl.ds(row, TILE)

        def hidden_tile(i, total):
            cols = pl.ds(pl.multiple_of(i * 512, 512), 512)
            h = tok[rows, cols].astype(F32)
            for g in range(4):
                h = h + dot(ctx[g, rows, :], wo[g, :, :, :, cols].reshape(COLS, 512))
            hid[:, cols] = h
            return total + jnp.sum(h * h, axis=-1, keepdims=True)

        total = lax.fori_loop(0, WIDTH // 512, hidden_tile, jnp.zeros((TILE, 1), F32))
        scale = lax.rsqrt(total * (1.0 / WIDTH) + EPS)

        @pl.loop(0, WIDTH // 256)
        def _(i):
            cols = pl.ds(pl.multiple_of(i * 256, 256), 256)
            nrm[pl.ds(0, TILE), cols] = (
                hid[:, cols] * scale * gain_c[:, cols].astype(F32)
            ).astype(BF16)

        acc[rows, :] = hid[:, pl.ds(pl.multiple_of(x * 512, 512), 512)]
        project(nrm.at[pl.ds(0, TILE)], wcq, cc, 0, 0.125)

        @pl.loop(0, COLS // 128)
        def _(pair):
            cols = pl.ds(pl.multiple_of(pair * 128, 128), 128)
            queries = cc[:, cols]
            halves_out = []
            for head in range(2):
                query = queries * pick[head]
                scores = [
                    dot_t(query, tk[block, pl.ds(tile * TILE, TILE), cols]) for tile in range(2)
                ]
                weights = softmax_parts(scores)
                mixed = None
                for tile in range(2):
                    term = dot(
                        weights[tile].astype(BF16),
                        with_ones(tv[block, pl.ds(tile * TILE, TILE), cols]),
                    )
                    mixed = term if mixed is None else mixed + term
                halves_out.append(ratio(mixed))
            cc[:, cols] = jnp.where(lane < 64, *halves_out).astype(BF16)

        def term(owner):
            cols = pl.ds(pl.multiple_of(owner * 512, 512), 512)
            return dot(cc[...], wco[:, cols]).astype(BF16)

        n = rs_n[c]
        part[c, 0] = term(across)
        send(part.at[c, 0, low], rs1.at[c, 0], to_right, n[0])
        send(part.at[c, 0, high], rs1.at[c, 1], to_left, n[1])
        part[c, 1] = term(right)
        send(part.at[c, 1, high], rs2.at[c, 0, high], to_right, n[2])
        part[c, 2] = term(left)
        send(part.at[c, 2, low], rs2.at[c, 1, low], to_left, n[3])
        acc[rows, :] = acc[rows, :] + term(x).astype(F32)

    def cross_middle(c):
        n = rs_n[c]
        landed(rs1.at[c, 0], n[0])
        fwd[c, 0] = (part[c, 1, low, :].astype(F32) + rs1[c, 0].astype(F32)).astype(BF16)
        send(fwd.at[c, 0], rs2.at[c, 0, low], to_right, n[4])
        landed(rs1.at[c, 1], n[1])
        fwd[c, 1] = (part[c, 2, high, :].astype(F32) + rs1[c, 1].astype(F32)).astype(BF16)
        send(fwd.at[c, 1], rs2.at[c, 1, high], to_left, n[5])

    stores = []

    def cross_end(c, block, half):
        n = rs_n[c]
        rows = pl.ds(block * BLK + half * TILE, TILE)
        landed(rs2.at[c, 0, high], n[2])
        landed(rs2.at[c, 1, low], n[3])
        landed(rs2.at[c, 0, low], n[4])
        landed(rs2.at[c, 1, high], n[5])
        ob[rows, :] = (acc[rows, :] + rs2[c, 0].astype(F32) + rs2[c, 1].astype(F32)).astype(BF16)
        copy = pltpu.make_async_copy(ob.at[rows], out.at[rows], lsem.at[len(loads) + c])
        copy.start()
        stores.append(copy)

    loaded("wo", "wcq", "wco")
    for g, n in zip(others, wo_n):
        landed(wo.at[g, 1 - core], n)
    for c, chunk in enumerate(CHUNKS):
        ctx_x[c].finish()
        cross_chunk(c, *chunk)
        if c >= 1:
            cross_middle(c - 1)
        if c >= 2:
            cross_end(c - 2, *CHUNKS[c - 2])
    last = len(CHUNKS) - 1
    cross_middle(last)
    cross_end(last - 1, *CHUNKS[last - 1])
    cross_end(last, *CHUNKS[last])
    for copy in sent:
        copy.wait_send()
    for copy in stores:
        copy.wait()


def on_device(
    tokens, gain_self, gain_cross, w_query, w_key, w_value, w_out, w_cross_query, w_cross_out,
    w_text_key, w_text_value, text_states, song_of_block, last_fill,
):
    any_space = pl.BlockSpec(memory_space=pl.ANY)
    vmem = pl.BlockSpec(memory_space=pltpu.VMEM)
    smem = pl.BlockSpec(memory_space=pltpu.SMEM)
    n = len(CHUNKS)

    def buf(*shape, dtype=BF16):
        return pltpu.VMEM(shape, dtype)

    scratch = [
        buf(1024, WIDTH),
        buf(BLK, WIDTH),
        buf(WIDTH, COLS),
        buf(WIDTH, COLS),
        buf(WIDTH, COLS),
        buf(4, 2, 4, 64, WIDTH),
        buf(WIDTH, COLS),
        buf(COLS, WIDTH),
        buf(1024, COLS),
        buf(1024, COLS),
        buf(2, 4, 128, 1024),
        buf(4, 128, 1024),
        buf(2, 128, 1024),
        buf(128, 1024),
        buf(1024, COLS),
        buf(1024, COLS),
        buf(1024, COLS),
        buf(BLK, COLS),
        buf(BLK, COLS),
        buf(4, 1024, COLS),
        buf(TILE, WIDTH, dtype=F32),
        buf(1024, COLS, dtype=F32),
        buf(n, 3, TILE, COLS),
        buf(n, 2, TILE // 2, COLS),
        buf(n, 2, TILE, COLS),
        buf(n, 2, TILE // 2, COLS),
        buf(2, BLK, COLS),
        buf(2, BLK, COLS),
        buf(TILE, BLK, dtype=F32),
        buf(TILE, COLS),
        buf(1024, COLS),
        pltpu.SemaphoreType.DMA((16,)),
        pltpu.SemaphoreType.DMA((REMOTE,)),
        pltpu.SemaphoreType.DMA((REMOTE,)),
    ]
    return pl.pallas_call(
        kernel,
        out_shape=jax.ShapeDtypeStruct((1024, COLS), BF16),
        in_specs=[any_space, vmem, vmem] + [any_space] * 9 + [smem, smem],
        out_specs=any_space,
        scratch_shapes=scratch,
        compiler_params=pltpu.CompilerParams(
            collective_id=0, has_side_effects=True, vmem_limit_bytes=62 * 2**20
        ),
    )(
        tokens, gain_self.reshape(1, WIDTH), gain_cross.reshape(1, WIDTH), w_query, w_key, w_value,
        w_out.reshape(2, 4, 64, WIDTH), w_cross_query, w_cross_out, w_text_key, w_text_value,
        text_states.reshape(2, 4, 128, 1024), song_of_block, last_fill,
    )


def solution(mesh):
    in_specs = (
        P("tm", None),
        P(),
        P(),
        P(None, "mp"),
        P(None, "mp"),
        P(None, "mp"),
        P("mp", None),
        P(None, "mp"),
        P("mp", None),
        P(None, "mp"),
        P(None, "mp"),
        P("tm", None, None),
        P(),
        P(),
    )
    return jax.shard_map(
        on_device, mesh=mesh, in_specs=in_specs, out_specs=P("tm", "mp"), check_vma=False
    )
```

```python
import jax
import jax.numpy as jnp
from jax import lax
from jax.experimental import pallas as pl
from jax.experimental.pallas import tpu as pltpu
from jax.sharding import PartitionSpec as P

F32 = jnp.float32
BF16 = jnp.bfloat16
EPS = 1e-05
MESH = pl.DeviceIdType.MESH
BLK = 512
TILE = 256
COLS = 512
WIDTH = 2048
SUB = TILE // 4
CHUNKS = ((1, 0), (1, 1), (0, 0), (0, 1))
REMOTE = 120


def dot(a, b):
    return jnp.dot(a, b, preferred_element_type=F32)


def dot_t(a, b):
    return lax.dot_general(a, b, (((1,), (1,)), ((), ())), preferred_element_type=F32)


def kernel(
    tokens, gain_s, gain_c, w_q, w_k, w_v, w_o, w_cq, w_co, w_tk, w_tv, text, song, fill,
    out,
    tok, nrm, wq, wk, wv, wo, wcq, wco, wtk, wtv, txt, tin, tsib,
    q, k, v, kp, vp, ctx, hid, own, cs, cr, os_, tk, tv, bias, cc,
    lsem, ssem, rsem,
):
    t, x = lax.axis_index("tm"), lax.axis_index("mp")
    core, y, z = lax.rem(t, 2), t // 8, lax.rem(t // 2, 4)
    right, left, across = lax.rem(x + 1, 4), lax.rem(x + 3, 4), lax.rem(x + 2, 4)
    to_right, to_left, to_across = {"mp": right}, {"mp": left}, {"mp": across}
    up, down = {"tm": lax.rem(t + 8, 32)}, {"tm": lax.rem(t + 24, 32)}
    z_up = {"tm": y * 8 + lax.rem(z + 1, 4) * 2 + core}
    z_down = {"tm": y * 8 + lax.rem(z + 3, 4) * 2 + core}
    next1, prev1 = {"tm": lax.rem(t + 1, 32)}, {"tm": lax.rem(t + 31, 32)}
    sibling = {"tm": t + 1 - 2 * core}

    loads = {}

    def load(name, src, dst):
        copy = pltpu.make_async_copy(src, dst, lsem.at[len(loads)])
        copy.start()
        loads[name] = copy

    def loaded(*names):
        for name in names:
            loads[name].wait()

    barrier = pltpu.get_barrier_semaphore()
    for peer in (prev1, to_right, to_left, to_across, up, down, z_up, z_down, sibling):
        pl.semaphore_signal(barrier, inc=1, device_id=peer, device_id_type=MESH)
    load("tok1", tokens.at[pl.ds(BLK, BLK)], tok.at[pl.ds(BLK, BLK)])
    load("wk", w_k, wk)
    load("wv", w_v, wv)
    load("wq", w_q, wq)
    load("tok0", tokens.at[pl.ds(0, BLK)], tok.at[pl.ds(0, BLK)])
    load("text", text, txt)
    load("wo", w_o, wo.at[x])
    load("wtk", w_tk, wtk)
    load("wtv", w_tv, wtv)
    load("wcq", w_cq, wcq)
    load("wco", w_co, wco.at[x])

    sent = []
    count = [0]

    def fresh():
        count[0] += 1
        return count[0] - 1

    def remote(src, dst, to, n):
        return pltpu.make_async_remote_copy(
            src_ref=src, dst_ref=dst, send_sem=ssem.at[n], recv_sem=rsem.at[n],
            device_id=to, device_id_type=MESH,
        )

    def send(src, dst, to, n):
        copy = remote(src, dst, to, n)
        copy.start()
        sent.append(copy)

    def landed(ref, n):
        remote(ref, ref, to_right, n).wait_recv()

    class Gather:
        def __init__(self, me, after, before, src, at):
            self.me, self.after, self.before, self.src, self.at = me, after, before, src, at
            self.n = [fresh() for _ in range(4)]

        def start(self):
            send(self.src, self.at(self.me, None), self.after, self.n[0])
            send(self.src, self.at(self.me, None), self.before, self.n[1])

        def forward(self):
            lo, hi = lax.rem(self.me + 3, 4), lax.rem(self.me + 1, 4)
            landed(self.at(lo, None), self.n[0])
            send(self.at(lo, 0), self.at(lo, 0), self.after, self.n[2])
            landed(self.at(hi, None), self.n[1])
            send(self.at(hi, 1), self.at(hi, 1), self.before, self.n[3])

        def finish(self):
            far = lax.rem(self.me + 2, 4)
            landed(self.at(far, 0), self.n[2])
            landed(self.at(far, 1), self.n[3])

    def halves(ref, half, size):
        return ref if half is None else ref.at[pl.ds(half * size, size)]

    class Whole:
        def __init__(self, src, full, me, after, before):
            self.full = full
            self.over_x = Gather(
                x, to_right, to_left, src.at[core, me],
                lambda i, h: halves(full.at[i, core, me], h, 32),
            )
            self.groups = (left, right, across)
            self.over_axis = [
                Gather(
                    me, after, before, full.at[g, core, me],
                    lambda i, h, g=g: halves(full.at[g, core, i], h, 32),
                )
                for g in self.groups
            ]
            self.n = [fresh() for _ in range(3)]

        def start(self):
            self.over_x.start()

        def second(self):
            self.over_x.forward()
            self.over_axis[0].start()
            self.over_axis[1].start()

        def third(self):
            self.over_x.finish()
            self.over_axis[2].start()

        def fourth(self, i):
            self.over_axis[i].forward()

        def fifth(self, i):
            self.over_axis[i].finish()
            rows = self.full.at[self.groups[i], core]
            send(rows, rows, sibling, self.n[i])

        def finish(self):
            for i in range(3):
                landed(self.full.at[self.groups[i], 1 - core], self.n[i])

    def strip(i):
        return pl.ds(pl.multiple_of(i * COLS, COLS), COLS)

    whole_o = Whole(w_o, wo, y, up, down)
    whole_co = Whole(w_co, wco, z, z_up, z_down)
    text_n = [fresh() for _ in range(2)]
    kv_n = [fresh() for _ in range(2)]
    ctx_x = [
        Gather(
            x, to_right, to_left, ctx.at[pl.ds(b * BLK + h * TILE, TILE), strip(x)],
            lambda i, part, r=b * BLK + h * TILE: (
                ctx.at[pl.ds(r, TILE), strip(i)]
                if part is None
                else ctx.at[pl.ds(r + part * TILE // 2, TILE // 2), strip(i)]
            ),
        )
        for b, h in CHUNKS
    ]
    cross_n = [[fresh() for _ in range(3)] for _ in CHUNKS]
    out_n = [[fresh() for _ in range(3)] for _ in CHUNKS]

    pl.semaphore_wait(barrier, 9)
    whole_o.start()
    send(text.at[1], tsib, sibling, text_n[0])

    b0 = 2 * t
    s0, s1 = song[b0], song[b0 + 1]
    m1 = song[jnp.maximum(b0 - 1, 0)]
    p2 = song[jnp.minimum(b0 + 2, 63)]
    same = [(t > 0) & (m1 == s0), s0 == s1]
    filled = [
        jnp.where(s0 != s1, fill[s0], BLK),
        jnp.where((t == 31) | (p2 != s1), fill[s1], BLK),
    ]

    def normed(block):
        gain = gain_s[...].astype(F32)

        @pl.loop(0, BLK // 32)
        def _(i):
            values = tok[pl.ds(pl.multiple_of(block * BLK + i * 32, 32), 32), :].astype(F32)
            meansq = jnp.mean(values * values, axis=-1, keepdims=True)
            nrm[pl.ds(pl.multiple_of(i * 32, 32), 32), :] = (
                values * lax.rsqrt(meansq + EPS) * gain
            ).astype(BF16)

    def project(a, w, dst, row, scale=None):
        res = dot(a[...], w[...]).astype(BF16)
        if scale is not None:
            res = res * jnp.asarray(scale, BF16)
        dst[pl.ds(row, a.shape[0]), :] = res

    loaded("tok1")
    normed(1)
    loaded("wk")
    project(nrm, wk, k, BLK)
    send(k.at[pl.ds(BLK, BLK)], kp, next1, kv_n[0])
    loaded("wv")
    project(nrm, wv, v, BLK)
    send(v.at[pl.ds(BLK, BLK)], vp, next1, kv_n[1])
    loaded("wq")
    project(nrm, wq, q, BLK, 0.125)
    whole_o.second()
    whole_co.start()
    loaded("tok0", "text")
    normed(0)
    landed(tsib, text_n[0])

    @pl.when(core == 1)
    def _():
        @pl.loop(0, 4)
        def _(i):
            tsib[i] = jnp.where(same[1], jnp.where(same[0], tsib[i], txt[0, i]), txt[1, i])

        remote(tsib, tin, next1, text_n[1]).start()

    project(nrm, wk, k, 0)
    project(nrm, wv, v, 0)
    whole_o.third()
    project(nrm, wq, q, 0, 0.125)

    lane = lax.broadcasted_iota(jnp.int32, (1, 128), 1)
    pick = [(lane < 64).astype(F32).astype(BF16), (lane >= 64).astype(F32).astype(BF16)]
    ones = jnp.ones((TILE, 128), BF16)

    def softmax_parts(tiles):
        top = tiles[0].max(axis=-1, keepdims=True)
        for s in tiles[1:]:
            top = jnp.maximum(top, s.max(axis=-1, keepdims=True))
        return [jnp.exp(s - top) for s in tiles]

    def with_ones(rows):
        return jnp.concatenate([rows, ones], axis=1)

    def ratio(mixed):
        return mixed[:, :128] / mixed[:, 128:]

    def self_chunk(block, half):
        row = block * BLK + half * TILE
        before_k, before_v = (k, v) if block == 1 else (kp, vp)
        i = lax.broadcasted_iota(jnp.int32, (TILE, BLK), 0) + half * TILE
        j = lax.broadcasted_iota(jnp.int32, (TILE, BLK), 1)
        limit = jnp.where(j <= i, filled[block], jnp.where(same[block], BLK, 0))
        bias[...] = jnp.where(j < limit, 0.0, -1e30)
        lower = lax.broadcasted_iota(jnp.int32, (TILE, TILE), 1) <= lax.broadcasted_iota(
            jnp.int32, (TILE, TILE), 0
        )

        for pair in range(COLS // 128):
            cols = pl.ds(pair * 128, 128)
            queries = q[pl.ds(row, TILE), cols]
            halves_out = []
            for head in range(2):
                query = queries * pick[head]
                scores = []
                for tile in range(2):
                    mine = pl.ds(block * BLK + tile * TILE, TILE)
                    earlier = pl.ds(tile * TILE, TILE)
                    if tile < half:
                        s = dot_t(query, k[mine, cols])
                    elif tile > half:
                        s = dot_t(query, before_k[earlier, cols])
                    else:
                        s = jnp.where(
                            lower,
                            dot_t(query, k[mine, cols]),
                            dot_t(query, before_k[earlier, cols]),
                        )
                    scores.append(s + bias[:, tile * TILE : (tile + 1) * TILE])
                weights = softmax_parts(scores)
                mixed = None
                for tile in range(2):
                    mine = pl.ds(block * BLK + tile * TILE, TILE)
                    earlier = pl.ds(tile * TILE, TILE)
                    w = weights[tile]
                    if tile < half:
                        terms = [(w, v[mine, cols])]
                    elif tile > half:
                        terms = [(w, before_v[earlier, cols])]
                    else:
                        terms = [
                            (jnp.where(lower, w, 0.0), v[mine, cols]),
                            (jnp.where(lower, 0.0, w), before_v[earlier, cols]),
                        ]
                    for a, b in terms:
                        term = dot(a.astype(BF16), with_ones(b))
                        mixed = term if mixed is None else mixed + term
                halves_out.append(ratio(mixed))
            ctx[pl.ds(row, TILE), pl.ds(pl.multiple_of(x * COLS + pair * 128, 128), 128)] = (
                jnp.where(lane < 64, *halves_out).astype(BF16)
            )

    self_chunk(*CHUNKS[0])
    ctx_x[0].start()
    whole_co.second()
    self_chunk(*CHUNKS[1])
    ctx_x[1].start()
    whole_o.fourth(0)
    whole_o.fourth(1)
    landed(kp, kv_n[0])
    landed(vp, kv_n[1])
    self_chunk(*CHUNKS[2])
    ctx_x[0].forward()
    ctx_x[2].start()
    whole_co.third()
    self_chunk(*CHUNKS[3])
    whole_o.fourth(2)
    whole_o.fifth(0)
    whole_o.fifth(1)
    ctx_x[1].forward()
    ctx_x[3].start()

    def choose():
        landed(tin, text_n[1])

        @pl.loop(0, 4)
        def _(i):
            first = jnp.where(same[0], tin[i], txt[0, i])
            txt[0, i] = first
            txt[1, i] = jnp.where(same[1], first, txt[1, i])

    @pl.when(core == 0)
    def _():
        choose()
        remote(txt.at[1], tin, next1, text_n[1]).start()

    whole_o.fifth(2)
    loaded("wo", "wcq")

    def hidden_chunk(c, block, half):
        row = block * BLK + half * TILE
        rows = pl.ds(row, TILE)
        total = jnp.zeros((TILE, 1), F32)
        for i in range(WIDTH // 512):
            cols = pl.ds(i * 512, 512)
            h = tok[rows, cols].astype(F32) + dot(
                ctx[rows, :], wo[:, :, :, :, cols].reshape(WIDTH, 512)
            )
            hid[:, cols] = h
            total = total + jnp.sum(h * h, axis=-1, keepdims=True)
        scale = lax.rsqrt(total * (1.0 / WIDTH) + EPS)
        for i in range(WIDTH // 512):
            cols = pl.ds(i * 512, 512)
            nrm[pl.ds(0, TILE), cols] = (
                hid[:, cols] * scale * gain_c[:, cols].astype(F32)
            ).astype(BF16)
        own[pl.ds(c * SUB, SUB), :] = hid[pl.ds(pl.multiple_of(x * SUB, SUB), SUB), :]
        project(nrm.at[pl.ds(0, TILE)], wcq, cc, 0, 0.125)

    def cross_chunk(c, block, half):
        for pair in range(COLS // 128):
            cols = pl.ds(pair * 128, 128)
            queries = cc[:, cols]
            halves_out = []
            for head in range(2):
                query = queries * pick[head]
                scores = [
                    dot_t(query, tk[block, pl.ds(tile * TILE, TILE), cols]) for tile in range(2)
                ]
                weights = softmax_parts(scores)
                mixed = None
                for tile in range(2):
                    term = dot(
                        weights[tile].astype(BF16),
                        with_ones(tv[block, pl.ds(tile * TILE, TILE), cols]),
                    )
                    mixed = term if mixed is None else mixed + term
                halves_out.append(ratio(mixed))
            cs[c, :, cols] = jnp.where(lane < 64, *halves_out).astype(BF16)
        sub = pl.ds(c * SUB, SUB)
        for to, owner, n in zip(
            (to_across, to_right, to_left), (across, right, left), cross_n[c]
        ):
            rows = pl.ds(pl.multiple_of(owner * SUB, SUB), SUB)
            send(cs.at[c, rows], cr.at[sub, strip(x)], to, n)
        cr[sub, strip(x)] = cs[c, pl.ds(pl.multiple_of(x * SUB, SUB), SUB), :]

    def out_rows(c):
        block, half = CHUNKS[c]
        row = pl.multiple_of(block * BLK + half * TILE + x * SUB, SUB)
        return pl.ds(row, SUB)

    def landing_rows(c, source):
        block, half = CHUNKS[c]
        return pl.ds(pl.multiple_of(block * BLK + half * TILE + source * SUB, SUB), SUB)

    stores = []

    def out_chunks(first, last):
        for c in range(first, last):
            for source, n in zip((across, left, right), cross_n[c]):
                landed(cr.at[pl.ds(c * SUB, SUB), strip(source)], n)
        rows = pl.ds(first * SUB, (last - first) * SUB)
        for d, to in ((2, to_across), (1, to_right), (3, to_left), (0, None)):
            cols = strip(lax.rem(x + d, 4))
            weight = wco[:, :, :, :, cols].reshape(WIDTH, COLS)
            os_[d, rows, :] = (own[rows, cols] + dot(cr[rows, :], weight)).astype(BF16)
            for c in range(first, last):
                piece = os_.at[d, pl.ds(c * SUB, SUB)]
                if to is None:
                    copy = pltpu.make_async_copy(
                        piece, out.at[out_rows(c)], lsem.at[len(loads) + c]
                    )
                    copy.start()
                    stores.append(copy)
                else:
                    send(piece, out.at[out_rows(c)], to, out_n[c][(2, 1, 3).index(d)])

    whole_o.finish()
    ctx_x[0].finish()
    hidden_chunk(0, *CHUNKS[0])
    ctx_x[2].forward()

    @pl.when(core == 1)
    def _():
        choose()

    loaded("wtk", "wtv")
    for block in (1, 0):
        rows = txt[block].reshape(BLK, 1024)
        tk[block] = dot(rows, wtk[...]).astype(BF16)
        tv[block] = dot(rows, wtv[...]).astype(BF16)
    for i in range(3):
        whole_co.fourth(i)
    cross_chunk(0, *CHUNKS[0])
    ctx_x[1].finish()
    hidden_chunk(1, *CHUNKS[1])
    ctx_x[3].forward()
    cross_chunk(1, *CHUNKS[1])
    for i in range(3):
        whole_co.fifth(i)
    ctx_x[2].finish()
    hidden_chunk(2, *CHUNKS[2])
    cross_chunk(2, *CHUNKS[2])
    loaded("wco")
    whole_co.finish()
    out_chunks(0, 2)
    ctx_x[3].finish()
    hidden_chunk(3, *CHUNKS[3])
    cross_chunk(3, *CHUNKS[3])
    out_chunks(2, 3)
    out_chunks(3, 4)
    for c in range(4):
        for source, n in zip((across, left, right), out_n[c]):
            landed(out.at[landing_rows(c, source)], n)
    for copy in sent:
        copy.wait_send()
    remote(tsib, tin, next1, text_n[1]).wait_send()
    for copy in stores:
        copy.wait()


def on_device(
    tokens, gain_self, gain_cross, w_query, w_key, w_value, w_out, w_cross_query, w_cross_out,
    w_text_key, w_text_value, text_states, song_of_block, last_fill,
):
    any_space = pl.BlockSpec(memory_space=pl.ANY)
    vmem = pl.BlockSpec(memory_space=pltpu.VMEM)
    smem = pl.BlockSpec(memory_space=pltpu.SMEM)
    n = len(CHUNKS)

    def buf(*shape, dtype=BF16):
        return pltpu.VMEM(shape, dtype)

    scratch = [
        buf(1024, WIDTH),
        buf(BLK, WIDTH),
        buf(WIDTH, COLS),
        buf(WIDTH, COLS),
        buf(WIDTH, COLS),
        buf(4, 2, 4, 64, WIDTH),
        buf(WIDTH, COLS),
        buf(4, 2, 4, 64, WIDTH),
        buf(1024, COLS),
        buf(1024, COLS),
        buf(2, 4, 128, 1024),
        buf(4, 128, 1024),
        buf(4, 128, 1024),
        buf(1024, COLS),
        buf(1024, COLS),
        buf(1024, COLS),
        buf(BLK, COLS),
        buf(BLK, COLS),
        buf(1024, WIDTH),
        buf(TILE, WIDTH, dtype=F32),
        buf(TILE, WIDTH, dtype=F32),
        buf(n, TILE, COLS),
        buf(TILE, WIDTH),
        buf(4, TILE, COLS),
        buf(2, BLK, COLS),
        buf(2, BLK, COLS),
        buf(TILE, BLK, dtype=F32),
        buf(TILE, COLS),
        pltpu.SemaphoreType.DMA((16,)),
        pltpu.SemaphoreType.DMA((REMOTE,)),
        pltpu.SemaphoreType.DMA((REMOTE,)),
    ]
    return pl.pallas_call(
        kernel,
        out_shape=jax.ShapeDtypeStruct((1024, COLS), BF16),
        in_specs=[any_space, vmem, vmem] + [any_space] * 9 + [smem, smem],
        out_specs=any_space,
        scratch_shapes=scratch,
        compiler_params=pltpu.CompilerParams(
            collective_id=0, has_side_effects=True, vmem_limit_bytes=62 * 2**20
        ),
    )(
        tokens, gain_self.reshape(1, WIDTH), gain_cross.reshape(1, WIDTH), w_query, w_key, w_value,
        w_out.reshape(2, 4, 64, WIDTH), w_cross_query, w_cross_out.reshape(2, 4, 64, WIDTH),
        w_text_key, w_text_value,
        text_states.reshape(2, 4, 128, 1024), song_of_block, last_fill,
    )


def solution(mesh):
    in_specs = (
        P("tm", None),
        P(),
        P(),
        P(None, "mp"),
        P(None, "mp"),
        P(None, "mp"),
        P("mp", None),
        P(None, "mp"),
        P("mp", None),
        P(None, "mp"),
        P(None, "mp"),
        P("tm", None, None),
        P(),
        P(),
    )
    return jax.shard_map(
        on_device, mesh=mesh, in_specs=in_specs, out_specs=P("tm", "mp"), check_vma=False
    )
```

```python
import jax
import jax.numpy as jnp
from jax import lax
from jax.experimental import pallas as pl
from jax.experimental.pallas import tpu as pltpu
from jax.sharding import PartitionSpec as P

F32 = jnp.float32
BF16 = jnp.bfloat16
EPS = 1e-05
MESH = pl.DeviceIdType.MESH
BLK = 512
TILE = 256
COLS = 512
WIDTH = 2048
SUB = TILE // 4
CHUNKS = ((1, 0), (1, 1), (0, 0), (0, 1))
FIRST_O = FIRST_CO = 1024
REMOTE = 192


def dot(a, b):
    return jnp.dot(a, b, preferred_element_type=F32)


def dot_t(a, b):
    return lax.dot_general(a, b, (((1,), (1,)), ((), ())), preferred_element_type=F32)


def kernel(
    tokens, gain_s, gain_c, w_q, w_k, w_v, w_o, w_cq, w_co, w_tk, w_tv, text, song, fill,
    out,
    tok, nrm, wq, wk, wv, wo, wcq, wco, wtk, wtv, txt, tin, tsib,
    q, k, v, kp, vp, ctx, hid, own, cs, cr, os_, tk, tv, bias, cc,
    lsem, ssem, rsem,
):
    t, x = lax.axis_index("tm"), lax.axis_index("mp")
    core, y, z = lax.rem(t, 2), t // 8, lax.rem(t // 2, 4)
    right, left, across = lax.rem(x + 1, 4), lax.rem(x + 3, 4), lax.rem(x + 2, 4)
    to_right, to_left, to_across = {"mp": right}, {"mp": left}, {"mp": across}
    y_up, y_down = {"tm": lax.rem(t + 8, 32)}, {"tm": lax.rem(t + 24, 32)}
    y_far = {"tm": lax.rem(t + 16, 32)}
    z_up = {"tm": y * 8 + lax.rem(z + 1, 4) * 2 + core}
    z_down = {"tm": y * 8 + lax.rem(z + 3, 4) * 2 + core}
    z_far = {"tm": y * 8 + lax.rem(z + 2, 4) * 2 + core}
    next1, prev1 = {"tm": lax.rem(t + 1, 32)}, {"tm": lax.rem(t + 31, 32)}
    sibling = {"tm": t + 1 - 2 * core}

    loads = {}

    def load(name, src, dst):
        copy = pltpu.make_async_copy(src, dst, lsem.at[len(loads)])
        copy.start()
        loads[name] = copy

    def loaded(*names):
        for name in names:
            loads[name].wait()

    barrier = pltpu.get_barrier_semaphore()
    peers = (prev1, to_right, to_left, to_across, y_up, y_down, y_far, z_up, z_down, z_far, sibling)
    for peer in peers:
        pl.semaphore_signal(barrier, inc=1, device_id=peer, device_id_type=MESH)
    load("tok1", tokens.at[pl.ds(BLK, BLK)], tok.at[pl.ds(BLK, BLK)])
    load("wk", w_k, wk)

    sent = []
    count = [0]

    def fresh():
        count[0] += 1
        return count[0] - 1

    def remote(src, dst, to, n):
        return pltpu.make_async_remote_copy(
            src_ref=src, dst_ref=dst, send_sem=ssem.at[n], recv_sem=rsem.at[n],
            device_id=to, device_id_type=MESH,
        )

    def send(src, dst, to, n):
        copy = remote(src, dst, to, n)
        copy.start()
        sent.append(copy)

    def landed(ref, n):
        remote(ref, ref, to_right, n).wait_recv()

    class Gather:
        def __init__(self, row):
            self.row = row
            self.n = [fresh() for _ in range(4)]

        def at(self, d, half=None):
            if half is None:
                return ctx.at[pl.ds(self.row, TILE), pl.ds(d * COLS, COLS)]
            rows = pl.ds(self.row + half * TILE // 2, TILE // 2)
            return ctx.at[rows, pl.ds(d * COLS, COLS)]

        def start(self):
            send(self.at(0), self.at(3), to_right, self.n[0])
            send(self.at(0), self.at(1), to_left, self.n[1])

        def forward(self):
            landed(self.at(3), self.n[0])
            send(self.at(3, 0), self.at(2, 0), to_right, self.n[2])
            landed(self.at(1), self.n[1])
            send(self.at(1, 1), self.at(2, 1), to_left, self.n[3])

        def finish(self):
            landed(self.at(2, 0), self.n[2])
            landed(self.at(2, 1), self.n[3])

    class Whole:
        def __init__(self, src, full, first):
            self.src, self.full = src, full
            self.n = iter([fresh() for _ in range(64)])
            self.parts = (
                (pl.ds(0, first), y, (y_up, y_down, y_far), z, (z_up, z_down)),
                (pl.ds(first, WIDTH - first), z, (z_up, z_down, z_far), y, (y_up, y_down)),
            )
            self.waits, self.late, self.last = [], ([], []), []

        def ref(self, part, axis, at_first, at_second):
            cols = self.parts[part][0]
            at_y, at_z = (at_first, at_second) if part == 0 else (at_second, at_first)
            return self.full.at[pl.ds(1, 3), core, at_y, at_z, :, cols]

        def send(self, src, dst, to):
            n = next(self.n)
            send(src, dst, to, n)
            return n

        def arrived(self):
            for ref, n in self.waits:
                landed(ref, n)
            self.waits = []

        def start(self):
            piece = self.src.at[core, y, z]
            for d, to in ((3, to_right), (1, to_left), (2, to_across)):
                spot = self.full.at[d, core, y, z]
                self.waits.append((spot, self.send(piece, spot, to)))

        def second(self):
            self.arrived()
            for i, (_, one, (up, down, far), two, _) in enumerate(self.parts):
                spot = self.ref(i, 0, one, two)
                for to, back in ((up, 3), (down, 1), (far, 2)):
                    n = self.send(spot, spot, to)
                    self.waits.append((self.ref(i, 0, lax.rem(one + back, 4), two), n))

        def third(self):
            self.arrived()
            for i, (_, _, _, two, (up, down)) in enumerate(self.parts):
                spot = self.ref(i, 1, pl.ds(0, 4), two)
                for to, back in ((up, 3), (down, 1)):
                    n = self.send(spot, spot, to)
                    self.waits.append((self.ref(i, 1, pl.ds(0, 4), lax.rem(two + back, 4)), n))

        def fourth(self, i):
            _, _, _, two, (up, down) = self.parts[i]
            for ref, n in self.waits[2 * i : 2 * i + 2]:
                landed(ref, n)
            far = lax.rem(two + 2, 4)
            for to, back, half in ((up, 3, pl.ds(0, 2)), (down, 1, pl.ds(2, 2))):
                spot = self.ref(i, 1, half, lax.rem(two + back, 4))
                n = self.send(spot, spot, to)
                self.late[i].append((self.ref(i, 1, half, far), n))
            for back in (0, 1, 3):
                self.share(i, lax.rem(two + back, 4))

        def share(self, i, at):
            at_y, at_z = (pl.ds(0, 4), at) if i == 0 else (at, pl.ds(0, 4))
            cols = self.parts[i][0]
            spot = self.full.at[pl.ds(1, 3), core, at_y, at_z, :, cols]
            n = self.send(spot, spot, sibling)
            self.last.append((self.full.at[pl.ds(1, 3), 1 - core, at_y, at_z, :, cols], n))

        def fifth(self, i):
            for ref, n in self.late[i]:
                landed(ref, n)
            self.share(i, lax.rem(self.parts[i][3] + 2, 4))

        def finish(self):
            for ref, n in self.last:
                landed(ref, n)

    def strip(i):
        return pl.ds(pl.multiple_of(i * COLS, COLS), COLS)

    whole_o = Whole(w_o, wo, FIRST_O)
    whole_co = Whole(w_co, wco, FIRST_CO)
    text_n = [fresh() for _ in range(6)]
    kv_n = [fresh() for _ in range(2)]
    ctx_x = [
        Gather(b * BLK + h * TILE)
        for b, h in CHUNKS
    ]
    cross_n = [[fresh() for _ in range(3)] for _ in CHUNKS]
    out_n = [[fresh() for _ in range(3)] for _ in CHUNKS]


    b0 = 2 * t
    s0, s1 = song[b0], song[b0 + 1]
    m1 = song[jnp.maximum(b0 - 1, 0)]
    p2 = song[jnp.minimum(b0 + 2, 63)]
    same = [(t > 0) & (m1 == s0), s0 == s1]
    filled = [
        jnp.where(s0 != s1, fill[s0], BLK),
        jnp.where((t == 31) | (p2 != s1), fill[s1], BLK),
    ]

    def normed(block):
        gain = gain_s[...].astype(F32).reshape(1, WIDTH)

        @pl.loop(0, BLK // 32)
        def _(i):
            values = tok[pl.ds(pl.multiple_of(block * BLK + i * 32, 32), 32), :].astype(F32)
            meansq = jnp.mean(values * values, axis=-1, keepdims=True)
            nrm[pl.ds(pl.multiple_of(i * 32, 32), 32), :] = (
                values * lax.rsqrt(meansq + EPS) * gain
            ).astype(BF16)

    def project(a, w, dst, row, scale=None):
        res = dot(a[...], w[...]).astype(BF16)
        if scale is not None:
            res = res * jnp.asarray(scale, BF16)
        dst[pl.ds(row, a.shape[0]), :] = res

    loaded("tok1")
    load("wv", w_v, wv)
    normed(1)
    loaded("wk")
    load("wq", w_q, wq)
    load("tok0", tokens.at[pl.ds(0, BLK)], tok.at[pl.ds(0, BLK)])
    project(nrm, wk, k, BLK)
    loaded("wv")
    load("text", text, txt)
    project(nrm, wv, v, BLK)
    pl.semaphore_wait(barrier, 11)
    whole_o.start()
    send(k.at[pl.ds(BLK, BLK)], kp, next1, kv_n[0])
    send(v.at[pl.ds(BLK, BLK)], vp, next1, kv_n[1])
    send(text.at[1], tsib, sibling, text_n[0])
    loaded("wq")
    project(nrm, wq, q, BLK, 0.125)
    loaded("tok0", "text")
    load("wo", w_o, wo.at[0])
    load("wtk", w_tk, wtk)
    load("wtv", w_tv, wtv)
    load("wcq", w_cq, wcq)
    load("wco", w_co, wco.at[0])
    normed(0)
    project(nrm, wk, k, 0)
    whole_o.second()
    whole_co.start()
    project(nrm, wv, v, 0)
    project(nrm, wq, q, 0, 0.125)

    lane = lax.broadcasted_iota(jnp.int32, (1, 128), 1)
    pick = [(lane < 64).astype(F32).astype(BF16), (lane >= 64).astype(F32).astype(BF16)]
    ones = jnp.ones((TILE, 128), BF16)

    def softmax_parts(tiles):
        top = tiles[0].max(axis=-1, keepdims=True)
        for s in tiles[1:]:
            top = jnp.maximum(top, s.max(axis=-1, keepdims=True))
        return [jnp.exp(s - top) for s in tiles]

    def with_ones(rows):
        return jnp.concatenate([rows, ones], axis=1)

    def ratio(mixed):
        return mixed[:, :128] / mixed[:, 128:]

    def self_chunk(block, half):
        row = block * BLK + half * TILE
        before_k, before_v = (k, v) if block == 1 else (kp, vp)
        i = lax.broadcasted_iota(jnp.int32, (TILE, BLK), 0) + half * TILE
        j = lax.broadcasted_iota(jnp.int32, (TILE, BLK), 1)
        limit = jnp.where(j <= i, filled[block], jnp.where(same[block], BLK, 0))
        bias[...] = jnp.where(j < limit, 0.0, -1e30)
        lower = lax.broadcasted_iota(jnp.int32, (TILE, TILE), 1) <= lax.broadcasted_iota(
            jnp.int32, (TILE, TILE), 0
        )

        for pair in range(COLS // 128):
            cols = pl.ds(pair * 128, 128)
            queries = q[pl.ds(row, TILE), cols]
            halves_out = []
            for head in range(2):
                query = queries * pick[head]
                scores = []
                for tile in range(2):
                    mine = pl.ds(block * BLK + tile * TILE, TILE)
                    earlier = pl.ds(tile * TILE, TILE)
                    if tile < half:
                        s = dot_t(query, k[mine, cols])
                    elif tile > half:
                        s = dot_t(query, before_k[earlier, cols])
                    else:
                        s = jnp.where(
                            lower,
                            dot_t(query, k[mine, cols]),
                            dot_t(query, before_k[earlier, cols]),
                        )
                    scores.append(s + bias[:, tile * TILE : (tile + 1) * TILE])
                weights = softmax_parts(scores)
                mixed = None
                for tile in range(2):
                    mine = pl.ds(block * BLK + tile * TILE, TILE)
                    earlier = pl.ds(tile * TILE, TILE)
                    w = weights[tile]
                    if tile < half:
                        terms = [(w, v[mine, cols])]
                    elif tile > half:
                        terms = [(w, before_v[earlier, cols])]
                    else:
                        terms = [
                            (jnp.where(lower, w, 0.0), v[mine, cols]),
                            (jnp.where(lower, 0.0, w), before_v[earlier, cols]),
                        ]
                    for a, b in terms:
                        term = dot(a.astype(BF16), with_ones(b))
                        mixed = term if mixed is None else mixed + term
                halves_out.append(ratio(mixed))
            ctx[pl.ds(row, TILE), cols] = jnp.where(lane < 64, *halves_out).astype(BF16)

    self_chunk(*CHUNKS[0])
    ctx_x[0].start()
    landed(tsib, text_n[0])

    @pl.when(core == 1)
    def _():
        piece = jnp.where(same[0], tsib[x], txt[0, x])
        tsib[x] = jnp.where(same[1], piece, txt[1, x])
        remote(tsib.at[x], tin.at[x], next1, text_n[1]).start()

    self_chunk(*CHUNKS[1])
    ctx_x[1].start()
    whole_o.third()
    landed(kp, kv_n[0])
    landed(vp, kv_n[1])
    self_chunk(*CHUNKS[2])
    ctx_x[2].start()

    @pl.when(core == 0)
    def _():
        landed(tin.at[x], text_n[1])
        for to, n in zip((to_across, to_right, to_left), text_n[2:]):
            remote(tin.at[x], tin.at[x], to, n).start()

    self_chunk(*CHUNKS[3])
    ctx_x[3].start()
    ctx_x[0].forward()
    whole_o.fourth(1)
    whole_o.fourth(0)
    whole_co.second()
    ctx_x[1].forward()
    whole_o.fifth(1)
    whole_o.fifth(0)
    ctx_x[2].forward()

    def choose():
        @pl.loop(0, 4)
        def _(i):
            first = jnp.where(same[0], tin[i], txt[0, i])
            txt[0, i] = first
            txt[1, i] = jnp.where(same[1], first, txt[1, i])

    @pl.when(core == 0)
    def _():
        for source, n in zip((across, left, right), text_n[2:]):
            landed(tin.at[source], n)
        choose()
        remote(txt.at[1], tin, sibling, text_n[5]).start()

    def hidden_chunk(c, block, half):
        row = block * BLK + half * TILE
        rows = pl.ds(row, TILE)
        total = jnp.zeros((TILE, 1), F32)
        for i in range(WIDTH // 512):
            cols = pl.ds(i * 512, 512)
            h = tok[rows, cols].astype(F32) + dot(
                ctx[rows, :], wo[:, :, :, :, :, cols].reshape(WIDTH, 512)
            )
            hid[:, cols] = h
            total = total + jnp.sum(h * h, axis=-1, keepdims=True)
        scale = lax.rsqrt(total * (1.0 / WIDTH) + EPS)
        for i in range(WIDTH // 512):
            cols = pl.ds(i * 512, 512)
            nrm[pl.ds(0, TILE), cols] = (
                hid[:, cols] * scale * gain_c[cols].astype(F32).reshape(1, 512)
            ).astype(BF16)
        own[pl.ds(c * SUB, SUB), :] = hid[pl.ds(pl.multiple_of(x * SUB, SUB), SUB), :]
        project(nrm.at[pl.ds(0, TILE)], wcq, cc, 0, 0.125)

    def cross_chunk(c, block, half):
        for pair in range(COLS // 128):
            cols = pl.ds(pair * 128, 128)
            queries = cc[:, cols]
            halves_out = []
            for head in range(2):
                query = queries * pick[head]
                scores = [
                    dot_t(query, tk[block, pl.ds(tile * TILE, TILE), cols]) for tile in range(2)
                ]
                weights = softmax_parts(scores)
                mixed = None
                for tile in range(2):
                    term = dot(
                        weights[tile].astype(BF16),
                        with_ones(tv[block, pl.ds(tile * TILE, TILE), cols]),
                    )
                    mixed = term if mixed is None else mixed + term
                halves_out.append(ratio(mixed))
            cs[c, :, cols] = jnp.where(lane < 64, *halves_out).astype(BF16)
        sub = pl.ds(c * SUB, SUB)
        for d, to, n in zip((2, 1, 3), (to_across, to_right, to_left), cross_n[c]):
            rows = pl.ds(pl.multiple_of(lax.rem(x + d, 4) * SUB, SUB), SUB)
            send(cs.at[c, rows], cr.at[sub, pl.ds((4 - d) * COLS, COLS)], to, n)
        cr[sub, pl.ds(0, COLS)] = cs[c, pl.ds(pl.multiple_of(x * SUB, SUB), SUB), :]

    def out_rows(c):
        block, half = CHUNKS[c]
        row = pl.multiple_of(block * BLK + half * TILE + x * SUB, SUB)
        return pl.ds(row, SUB)

    def landing_rows(c, source):
        block, half = CHUNKS[c]
        return pl.ds(pl.multiple_of(block * BLK + half * TILE + source * SUB, SUB), SUB)

    stores = []

    def out_chunks(first, last):
        for c in range(first, last):
            for d, n in zip((2, 3, 1), cross_n[c]):
                landed(cr.at[pl.ds(c * SUB, SUB), pl.ds(d * COLS, COLS)], n)
        rows = pl.ds(first * SUB, (last - first) * SUB)
        for d, to in ((2, to_across), (1, to_right), (3, to_left), (0, None)):
            cols = strip(lax.rem(x + d, 4))
            weight = wco[:, :, :, :, :, cols].reshape(WIDTH, COLS)
            os_[d, rows, :] = (own[rows, cols] + dot(cr[rows, :], weight)).astype(BF16)
            for c in range(first, last):
                piece = os_.at[d, pl.ds(c * SUB, SUB)]
                if to is None:
                    copy = pltpu.make_async_copy(
                        piece, out.at[out_rows(c)], lsem.at[len(loads) + c]
                    )
                    copy.start()
                    stores.append(copy)
                else:
                    send(piece, out.at[out_rows(c)], to, out_n[c][(2, 1, 3).index(d)])

    whole_co.third()
    ctx_x[3].forward()

    @pl.when(core == 1)
    def _():
        landed(tin, text_n[5])
        choose()

    loaded("wtk", "wtv")
    for block in (1, 0):
        rows = txt[block].reshape(BLK, 1024)
        tk[block] = dot(rows, wtk[...]).astype(BF16)
        tv[block] = dot(rows, wtv[...]).astype(BF16)
    loaded("wo", "wcq")
    whole_o.finish()
    ctx_x[0].finish()
    hidden_chunk(0, *CHUNKS[0])
    cross_chunk(0, *CHUNKS[0])
    whole_co.fourth(1)
    whole_co.fourth(0)
    ctx_x[1].finish()
    hidden_chunk(1, *CHUNKS[1])
    cross_chunk(1, *CHUNKS[1])
    whole_co.fifth(1)
    whole_co.fifth(0)
    ctx_x[2].finish()
    hidden_chunk(2, *CHUNKS[2])
    cross_chunk(2, *CHUNKS[2])
    loaded("wco")
    whole_co.finish()
    out_chunks(0, 2)
    ctx_x[3].finish()
    hidden_chunk(3, *CHUNKS[3])
    cross_chunk(3, *CHUNKS[3])
    out_chunks(2, 3)
    out_chunks(3, 4)
    for c in range(4):
        for source, n in zip((across, left, right), out_n[c]):
            landed(out.at[landing_rows(c, source)], n)
    for copy in sent:
        copy.wait_send()

    @pl.when(core == 1)
    def _():
        remote(tsib.at[x], tin.at[x], next1, text_n[1]).wait_send()

    @pl.when(core == 0)
    def _():
        for to, n in zip((to_across, to_right, to_left), text_n[2:]):
            remote(tin.at[x], tin.at[x], to, n).wait_send()
        remote(txt.at[1], tin, sibling, text_n[5]).wait_send()

    for copy in stores:
        copy.wait()


def on_device(
    tokens, gain_self, gain_cross, w_query, w_key, w_value, w_out, w_cross_query, w_cross_out,
    w_text_key, w_text_value, text_states, song_of_block, last_fill,
):
    any_space = pl.BlockSpec(memory_space=pl.ANY)
    vmem = pl.BlockSpec(memory_space=pltpu.VMEM)
    smem = pl.BlockSpec(memory_space=pltpu.SMEM)
    n = len(CHUNKS)

    def buf(*shape, dtype=BF16):
        return pltpu.VMEM(shape, dtype)

    scratch = [
        buf(1024, WIDTH),
        buf(BLK, WIDTH),
        buf(WIDTH, COLS),
        buf(WIDTH, COLS),
        buf(WIDTH, COLS),
        buf(4, 2, 4, 4, 16, WIDTH),
        buf(WIDTH, COLS),
        buf(4, 2, 4, 4, 16, WIDTH),
        buf(1024, COLS),
        buf(1024, COLS),
        buf(2, 4, 128, 1024),
        buf(4, 128, 1024),
        buf(4, 128, 1024),
        buf(1024, COLS),
        buf(1024, COLS),
        buf(1024, COLS),
        buf(BLK, COLS),
        buf(BLK, COLS),
        buf(1024, WIDTH),
        buf(TILE, WIDTH, dtype=F32),
        buf(TILE, WIDTH, dtype=F32),
        buf(n, TILE, COLS),
        buf(TILE, WIDTH),
        buf(4, TILE, COLS),
        buf(2, BLK, COLS),
        buf(2, BLK, COLS),
        buf(TILE, BLK, dtype=F32),
        buf(TILE, COLS),
        pltpu.SemaphoreType.DMA((16,)),
        pltpu.SemaphoreType.DMA((REMOTE,)),
        pltpu.SemaphoreType.DMA((REMOTE,)),
    ]
    return pl.pallas_call(
        kernel,
        out_shape=jax.ShapeDtypeStruct((1024, COLS), BF16),
        in_specs=[any_space, vmem, vmem] + [any_space] * 9 + [smem, smem],
        out_specs=any_space,
        scratch_shapes=scratch,
        compiler_params=pltpu.CompilerParams(
            collective_id=0, has_side_effects=True, vmem_limit_bytes=62 * 2**20
        ),
    )(
        tokens, gain_self, gain_cross, w_query, w_key, w_value,
        w_out.reshape(2, 4, 4, 16, WIDTH), w_cross_query, w_cross_out.reshape(2, 4, 4, 16, WIDTH),
        w_text_key, w_text_value,
        text_states.reshape(2, 4, 128, 1024), song_of_block, last_fill,
    )


def solution(mesh):
    in_specs = (
        P("tm", None),
        P(),
        P(),
        P(None, "mp"),
        P(None, "mp"),
        P(None, "mp"),
        P("mp", None),
        P(None, "mp"),
        P("mp", None),
        P(None, "mp"),
        P(None, "mp"),
        P("tm", None, None),
        P(),
        P(),
    )
    return jax.shard_map(
        on_device, mesh=mesh, in_specs=in_specs, out_specs=P("tm", "mp"), check_vma=False
    )
```

```python
import jax
import jax.numpy as jnp
from jax import lax
from jax.experimental import pallas as pl
from jax.experimental.pallas import tpu as pltpu
from jax.sharding import PartitionSpec as P

F32 = jnp.float32
BF16 = jnp.bfloat16
EPS = 1e-05
MESH = pl.DeviceIdType.MESH
BLK = 512
TILE = 256
COLS = 512
WIDTH = 2048
SUB = TILE // 4
CHUNKS = ((1, 0), (1, 1), (0, 0), (0, 1))
FIRST_O, FIRST_CO = 1280, 1024
REMOTE = 192


def dot(a, b):
    return jnp.dot(a, b, preferred_element_type=F32)


def dot_t(a, b):
    return lax.dot_general(a, b, (((1,), (1,)), ((), ())), preferred_element_type=F32)


def kernel(
    tokens, gain_s, gain_c, w_q, w_k, w_v, w_o, w_cq, w_co, w_tk, w_tv, text, song, fill,
    out,
    tok, nrm, wq, wk, wv, wo, wcq, wco, wtk, wtv, txt, tin, tsib,
    q, k, v, kp, vp, ctx, hid, own, cs, cr, os_, tk, tv, bias, cc,
    lsem, ssem, rsem,
):
    t, x = lax.axis_index("tm"), lax.axis_index("mp")
    core, y, z = lax.rem(t, 2), t // 8, lax.rem(t // 2, 4)
    right, left, across = lax.rem(x + 1, 4), lax.rem(x + 3, 4), lax.rem(x + 2, 4)
    to_right, to_left, to_across = {"mp": right}, {"mp": left}, {"mp": across}
    y_up, y_down = {"tm": lax.rem(t + 8, 32)}, {"tm": lax.rem(t + 24, 32)}
    y_far = {"tm": lax.rem(t + 16, 32)}
    z_up = {"tm": y * 8 + lax.rem(z + 1, 4) * 2 + core}
    z_down = {"tm": y * 8 + lax.rem(z + 3, 4) * 2 + core}
    z_far = {"tm": y * 8 + lax.rem(z + 2, 4) * 2 + core}
    next1, prev1 = {"tm": lax.rem(t + 1, 32)}, {"tm": lax.rem(t + 31, 32)}
    sibling = {"tm": t + 1 - 2 * core}

    loads = {}

    def load(name, src, dst):
        copy = pltpu.make_async_copy(src, dst, lsem.at[len(loads)])
        copy.start()
        loads[name] = copy

    def loaded(*names):
        for name in names:
            loads[name].wait()

    barrier = pltpu.get_barrier_semaphore()
    peers = (prev1, to_right, to_left, to_across, y_up, y_down, y_far, z_up, z_down, z_far, sibling)
    for peer in peers:
        pl.semaphore_signal(barrier, inc=1, device_id=peer, device_id_type=MESH)
    load("tok1", tokens.at[pl.ds(BLK, BLK)], tok.at[pl.ds(BLK, BLK)])
    load("wk", w_k, wk)

    sent = []
    count = [0]

    def fresh():
        count[0] += 1
        return count[0] - 1

    def remote(src, dst, to, n):
        return pltpu.make_async_remote_copy(
            src_ref=src, dst_ref=dst, send_sem=ssem.at[n], recv_sem=rsem.at[n],
            device_id=to, device_id_type=MESH,
        )

    def send(src, dst, to, n):
        copy = remote(src, dst, to, n)
        copy.start()
        sent.append(copy)

    def landed(ref, n):
        remote(ref, ref, to_right, n).wait_recv()

    class Gather:
        def __init__(self, row):
            self.row = row
            self.n = [fresh() for _ in range(4)]

        def at(self, d, half=None):
            if half is None:
                return ctx.at[pl.ds(self.row, TILE), pl.ds(d * COLS, COLS)]
            rows = pl.ds(self.row + half * TILE // 2, TILE // 2)
            return ctx.at[rows, pl.ds(d * COLS, COLS)]

        def start(self):
            send(self.at(0), self.at(3), to_right, self.n[0])
            send(self.at(0), self.at(1), to_left, self.n[1])

        def forward(self):
            landed(self.at(3), self.n[0])
            send(self.at(3, 0), self.at(2, 0), to_right, self.n[2])
            landed(self.at(1), self.n[1])
            send(self.at(1, 1), self.at(2, 1), to_left, self.n[3])

        def finish(self):
            landed(self.at(2, 0), self.n[2])
            landed(self.at(2, 1), self.n[3])

    class Whole:
        def __init__(self, src, full, first):
            self.src, self.full = src, full
            self.n = iter([fresh() for _ in range(64)])
            self.parts = (
                (pl.ds(0, first), y, (y_up, y_down, y_far), z, (z_up, z_down)),
                (pl.ds(first, WIDTH - first), z, (z_up, z_down, z_far), y, (y_up, y_down)),
            )
            self.waits, self.late, self.last = [], ([], []), []

        def ref(self, part, axis, at_first, at_second):
            cols = self.parts[part][0]
            at_y, at_z = (at_first, at_second) if part == 0 else (at_second, at_first)
            return self.full.at[pl.ds(1, 3), core, at_y, at_z, :, cols]

        def send(self, src, dst, to):
            n = next(self.n)
            send(src, dst, to, n)
            return n

        def arrived(self):
            for ref, n in self.waits:
                landed(ref, n)
            self.waits = []

        def start(self):
            piece = self.src.at[core, y, z]
            for d, to in ((3, to_right), (1, to_left), (2, to_across)):
                spot = self.full.at[d, core, y, z]
                self.waits.append((spot, self.send(piece, spot, to)))

        def second(self):
            self.arrived()
            for i, (_, one, (up, down, far), two, _) in enumerate(self.parts):
                spot = self.ref(i, 0, one, two)
                for to, back in ((up, 3), (down, 1), (far, 2)):
                    n = self.send(spot, spot, to)
                    self.waits.append((self.ref(i, 0, lax.rem(one + back, 4), two), n))

        def third(self):
            self.arrived()
            for i, (_, _, _, two, (up, down)) in enumerate(self.parts):
                spot = self.ref(i, 1, pl.ds(0, 4), two)
                for to, back in ((up, 3), (down, 1)):
                    n = self.send(spot, spot, to)
                    self.waits.append((self.ref(i, 1, pl.ds(0, 4), lax.rem(two + back, 4)), n))

        def fourth(self, i):
            _, _, _, two, (up, down) = self.parts[i]
            for ref, n in self.waits[2 * i : 2 * i + 2]:
                landed(ref, n)
            far = lax.rem(two + 2, 4)
            for to, back, half in ((up, 3, pl.ds(0, 2)), (down, 1, pl.ds(2, 2))):
                spot = self.ref(i, 1, half, lax.rem(two + back, 4))
                n = self.send(spot, spot, to)
                self.late[i].append((self.ref(i, 1, half, far), n))
            for back in (0, 1, 3):
                self.share(i, lax.rem(two + back, 4))

        def share(self, i, at):
            at_y, at_z = (pl.ds(0, 4), at) if i == 0 else (at, pl.ds(0, 4))
            cols = self.parts[i][0]
            spot = self.full.at[pl.ds(1, 3), core, at_y, at_z, :, cols]
            n = self.send(spot, spot, sibling)
            self.last.append((self.full.at[pl.ds(1, 3), 1 - core, at_y, at_z, :, cols], n))

        def fifth(self, i):
            for ref, n in self.late[i]:
                landed(ref, n)
            self.share(i, lax.rem(self.parts[i][3] + 2, 4))

        def finish(self):
            for ref, n in self.last:
                landed(ref, n)

    def strip(i):
        return pl.ds(pl.multiple_of(i * COLS, COLS), COLS)

    whole_o = Whole(w_o, wo, FIRST_O)
    whole_co = Whole(w_co, wco, FIRST_CO)
    text_n = [fresh() for _ in range(6)]
    kv_n = [fresh() for _ in range(2)]
    ctx_x = [
        Gather(b * BLK + h * TILE)
        for b, h in CHUNKS
    ]
    cross_n = [[fresh() for _ in range(3)] for _ in CHUNKS]
    out_n = [[fresh() for _ in range(3)] for _ in CHUNKS]


    b0 = 2 * t
    s0, s1 = song[b0], song[b0 + 1]
    m1 = song[jnp.maximum(b0 - 1, 0)]
    p2 = song[jnp.minimum(b0 + 2, 63)]
    same = [(t > 0) & (m1 == s0), s0 == s1]
    filled = [
        jnp.where(s0 != s1, fill[s0], BLK),
        jnp.where((t == 31) | (p2 != s1), fill[s1], BLK),
    ]

    def normed(block):
        gain = gain_s[...].astype(F32).reshape(1, WIDTH)

        @pl.loop(0, BLK // 32)
        def _(i):
            values = tok[pl.ds(pl.multiple_of(block * BLK + i * 32, 32), 32), :].astype(F32)
            meansq = jnp.mean(values * values, axis=-1, keepdims=True)
            nrm[pl.ds(pl.multiple_of(i * 32, 32), 32), :] = (
                values * lax.rsqrt(meansq + EPS) * gain
            ).astype(BF16)

    def project(a, w, dst, row, scale=None):
        res = dot(a[...], w[...]).astype(BF16)
        if scale is not None:
            res = res * jnp.asarray(scale, BF16)
        dst[pl.ds(row, a.shape[0]), :] = res

    loaded("tok1")
    load("wv", w_v, wv)
    normed(1)
    loaded("wk")
    load("wq", w_q, wq)
    load("tok0", tokens.at[pl.ds(0, BLK)], tok.at[pl.ds(0, BLK)])
    project(nrm, wk, k, BLK)
    loaded("wv")
    load("text", text, txt)
    pl.semaphore_wait(barrier, 11)
    whole_o.start()
    send(k.at[pl.ds(BLK, BLK)], kp, next1, kv_n[0])
    project(nrm, wv, v, BLK)
    send(v.at[pl.ds(BLK, BLK)], vp, next1, kv_n[1])
    send(text.at[1], tsib, sibling, text_n[0])
    loaded("wq")
    project(nrm, wq, q, BLK, 0.125)
    loaded("tok0", "text")
    load("wo", w_o, wo.at[0])
    load("wtk", w_tk, wtk)
    load("wtv", w_tv, wtv)
    load("wcq", w_cq, wcq)
    load("wco", w_co, wco.at[0])
    normed(0)
    project(nrm, wk, k, 0)
    whole_o.second()
    whole_co.start()
    project(nrm, wv, v, 0)
    project(nrm, wq, q, 0, 0.125)

    lane = lax.broadcasted_iota(jnp.int32, (1, 128), 1)
    pick = [(lane < 64).astype(F32).astype(BF16), (lane >= 64).astype(F32).astype(BF16)]
    ones = jnp.ones((TILE, 128), BF16)

    def softmax_parts(tiles):
        top = tiles[0].max(axis=-1, keepdims=True)
        for s in tiles[1:]:
            top = jnp.maximum(top, s.max(axis=-1, keepdims=True))
        return [jnp.exp(s - top) for s in tiles]

    def with_ones(rows):
        return jnp.concatenate([rows, ones], axis=1)

    def ratio(mixed):
        return mixed[:, :128] / mixed[:, 128:]

    def self_chunk(block, half):
        row = block * BLK + half * TILE
        before_k, before_v = (k, v) if block == 1 else (kp, vp)
        i = lax.broadcasted_iota(jnp.int32, (TILE, BLK), 0) + half * TILE
        j = lax.broadcasted_iota(jnp.int32, (TILE, BLK), 1)
        limit = jnp.where(j <= i, filled[block], jnp.where(same[block], BLK, 0))
        bias[...] = jnp.where(j < limit, 0.0, -1e30)
        lower = lax.broadcasted_iota(jnp.int32, (TILE, TILE), 1) <= lax.broadcasted_iota(
            jnp.int32, (TILE, TILE), 0
        )

        for pair in range(COLS // 128):
            cols = pl.ds(pair * 128, 128)
            queries = q[pl.ds(row, TILE), cols]
            halves_out = []
            for head in range(2):
                query = queries * pick[head]
                scores = []
                for tile in range(2):
                    mine = pl.ds(block * BLK + tile * TILE, TILE)
                    earlier = pl.ds(tile * TILE, TILE)
                    if tile < half:
                        s = dot_t(query, k[mine, cols])
                    elif tile > half:
                        s = dot_t(query, before_k[earlier, cols])
                    else:
                        s = jnp.where(
                            lower,
                            dot_t(query, k[mine, cols]),
                            dot_t(query, before_k[earlier, cols]),
                        )
                    scores.append(s + bias[:, tile * TILE : (tile + 1) * TILE])
                weights = softmax_parts(scores)
                mixed = None
                for tile in range(2):
                    mine = pl.ds(block * BLK + tile * TILE, TILE)
                    earlier = pl.ds(tile * TILE, TILE)
                    w = weights[tile]
                    if tile < half:
                        terms = [(w, v[mine, cols])]
                    elif tile > half:
                        terms = [(w, before_v[earlier, cols])]
                    else:
                        terms = [
                            (jnp.where(lower, w, 0.0), v[mine, cols]),
                            (jnp.where(lower, 0.0, w), before_v[earlier, cols]),
                        ]
                    for a, b in terms:
                        term = dot(a.astype(BF16), with_ones(b))
                        mixed = term if mixed is None else mixed + term
                halves_out.append(ratio(mixed))
            ctx[pl.ds(row, TILE), cols] = jnp.where(lane < 64, *halves_out).astype(BF16)

    self_chunk(*CHUNKS[0])
    ctx_x[0].start()
    landed(tsib, text_n[0])

    @pl.when(core == 1)
    def _():
        piece = jnp.where(same[0], tsib[x], txt[0, x])
        tsib[x] = jnp.where(same[1], piece, txt[1, x])
        remote(tsib.at[x], tin.at[x], next1, text_n[1]).start()

    self_chunk(*CHUNKS[1])
    ctx_x[1].start()
    whole_o.third()
    landed(kp, kv_n[0])
    landed(vp, kv_n[1])
    self_chunk(*CHUNKS[2])
    ctx_x[2].start()

    @pl.when(core == 0)
    def _():
        landed(tin.at[x], text_n[1])
        for to, n in zip((to_across, to_right, to_left), text_n[2:]):
            remote(tin.at[x], tin.at[x], to, n).start()

    self_chunk(*CHUNKS[3])
    ctx_x[3].start()
    ctx_x[0].forward()
    whole_o.fourth(1)
    whole_o.fourth(0)
    whole_co.second()
    ctx_x[1].forward()
    whole_o.fifth(1)
    whole_o.fifth(0)
    ctx_x[2].forward()

    def choose():
        @pl.loop(0, 4)
        def _(i):
            first = jnp.where(same[0], tin[i], txt[0, i])
            txt[0, i] = first
            txt[1, i] = jnp.where(same[1], first, txt[1, i])

    @pl.when(core == 0)
    def _():
        for source, n in zip((across, left, right), text_n[2:]):
            landed(tin.at[source], n)
        choose()
        remote(txt.at[1], tin, sibling, text_n[5]).start()

    def hidden_chunk(c, block, half):
        row = block * BLK + half * TILE
        rows = pl.ds(row, TILE)
        total = jnp.zeros((TILE, 1), F32)
        for i in range(WIDTH // 512):
            cols = pl.ds(i * 512, 512)
            h = tok[rows, cols].astype(F32) + dot(
                ctx[rows, :], wo[:, :, :, :, :, cols].reshape(WIDTH, 512)
            )
            hid[:, cols] = h
            total = total + jnp.sum(h * h, axis=-1, keepdims=True)
        scale = lax.rsqrt(total * (1.0 / WIDTH) + EPS)
        for i in range(WIDTH // 512):
            cols = pl.ds(i * 512, 512)
            nrm[pl.ds(0, TILE), cols] = (
                hid[:, cols] * scale * gain_c[cols].astype(F32).reshape(1, 512)
            ).astype(BF16)
        own[pl.ds(c * SUB, SUB), :] = hid[pl.ds(pl.multiple_of(x * SUB, SUB), SUB), :]
        project(nrm.at[pl.ds(0, TILE)], wcq, cc, 0, 0.125)

    def cross_chunk(c, block, half):
        for pair in range(COLS // 128):
            cols = pl.ds(pair * 128, 128)
            queries = cc[:, cols]
            halves_out = []
            for head in range(2):
                query = queries * pick[head]
                scores = [
                    dot_t(query, tk[block, pl.ds(tile * TILE, TILE), cols]) for tile in range(2)
                ]
                weights = softmax_parts(scores)
                mixed = None
                for tile in range(2):
                    term = dot(
                        weights[tile].astype(BF16),
                        with_ones(tv[block, pl.ds(tile * TILE, TILE), cols]),
                    )
                    mixed = term if mixed is None else mixed + term
                halves_out.append(ratio(mixed))
            cs[c, :, cols] = jnp.where(lane < 64, *halves_out).astype(BF16)
        sub = pl.ds(c * SUB, SUB)
        for d, to, n in zip((2, 1, 3), (to_across, to_right, to_left), cross_n[c]):
            rows = pl.ds(pl.multiple_of(lax.rem(x + d, 4) * SUB, SUB), SUB)
            send(cs.at[c, rows], cr.at[sub, pl.ds((4 - d) * COLS, COLS)], to, n)
        cr[sub, pl.ds(0, COLS)] = cs[c, pl.ds(pl.multiple_of(x * SUB, SUB), SUB), :]

    def out_rows(c):
        block, half = CHUNKS[c]
        row = pl.multiple_of(block * BLK + half * TILE + x * SUB, SUB)
        return pl.ds(row, SUB)

    def landing_rows(c, source):
        block, half = CHUNKS[c]
        return pl.ds(pl.multiple_of(block * BLK + half * TILE + source * SUB, SUB), SUB)

    stores = []

    def out_chunks(first, last):
        for c in range(first, last):
            for d, n in zip((2, 3, 1), cross_n[c]):
                landed(cr.at[pl.ds(c * SUB, SUB), pl.ds(d * COLS, COLS)], n)
        rows = pl.ds(first * SUB, (last - first) * SUB)
        for d, to in ((2, to_across), (1, to_right), (3, to_left), (0, None)):
            cols = strip(lax.rem(x + d, 4))
            weight = wco[:, :, :, :, :, cols].reshape(WIDTH, COLS)
            os_[d, rows, :] = (own[rows, cols] + dot(cr[rows, :], weight)).astype(BF16)
            for c in range(first, last):
                piece = os_.at[d, pl.ds(c * SUB, SUB)]
                if to is None:
                    copy = pltpu.make_async_copy(
                        piece, out.at[out_rows(c)], lsem.at[len(loads) + c]
                    )
                    copy.start()
                    stores.append(copy)
                else:
                    send(piece, out.at[out_rows(c)], to, out_n[c][(2, 1, 3).index(d)])

    @pl.when(core == 1)
    def _():
        landed(tin, text_n[5])
        choose()

    loaded("wtk", "wtv")
    for block in (1, 0):
        rows = txt[block].reshape(BLK, 1024)
        tk[block] = dot(rows, wtk[...]).astype(BF16)
        tv[block] = dot(rows, wtv[...]).astype(BF16)
    whole_co.third()
    loaded("wo", "wcq")
    whole_o.finish()
    ctx_x[0].finish()
    hidden_chunk(0, *CHUNKS[0])
    ctx_x[3].forward()
    cross_chunk(0, *CHUNKS[0])
    ctx_x[1].finish()
    hidden_chunk(1, *CHUNKS[1])
    cross_chunk(1, *CHUNKS[1])
    whole_co.fourth(1)
    whole_co.fourth(0)
    ctx_x[2].finish()
    hidden_chunk(2, *CHUNKS[2])
    cross_chunk(2, *CHUNKS[2])
    whole_co.fifth(1)
    whole_co.fifth(0)
    ctx_x[3].finish()
    hidden_chunk(3, *CHUNKS[3])
    loaded("wco")
    whole_co.finish()
    out_chunks(0, 2)
    cross_chunk(3, *CHUNKS[3])
    out_chunks(2, 3)
    out_chunks(3, 4)
    for c in range(4):
        for source, n in zip((across, left, right), out_n[c]):
            landed(out.at[landing_rows(c, source)], n)
    for copy in sent:
        copy.wait_send()

    @pl.when(core == 1)
    def _():
        remote(tsib.at[x], tin.at[x], next1, text_n[1]).wait_send()

    @pl.when(core == 0)
    def _():
        for to, n in zip((to_across, to_right, to_left), text_n[2:]):
            remote(tin.at[x], tin.at[x], to, n).wait_send()
        remote(txt.at[1], tin, sibling, text_n[5]).wait_send()

    for copy in stores:
        copy.wait()


def on_device(
    tokens, gain_self, gain_cross, w_query, w_key, w_value, w_out, w_cross_query, w_cross_out,
    w_text_key, w_text_value, text_states, song_of_block, last_fill,
):
    any_space = pl.BlockSpec(memory_space=pl.ANY)
    vmem = pl.BlockSpec(memory_space=pltpu.VMEM)
    smem = pl.BlockSpec(memory_space=pltpu.SMEM)
    n = len(CHUNKS)

    def buf(*shape, dtype=BF16):
        return pltpu.VMEM(shape, dtype)

    scratch = [
        buf(1024, WIDTH),
        buf(BLK, WIDTH),
        buf(WIDTH, COLS),
        buf(WIDTH, COLS),
        buf(WIDTH, COLS),
        buf(4, 2, 4, 4, 16, WIDTH),
        buf(WIDTH, COLS),
        buf(4, 2, 4, 4, 16, WIDTH),
        buf(1024, COLS),
        buf(1024, COLS),
        buf(2, 4, 128, 1024),
        buf(4, 128, 1024),
        buf(4, 128, 1024),
        buf(1024, COLS),
        buf(1024, COLS),
        buf(1024, COLS),
        buf(BLK, COLS),
        buf(BLK, COLS),
        buf(1024, WIDTH),
        buf(TILE, WIDTH, dtype=F32),
        buf(TILE, WIDTH, dtype=F32),
        buf(n, TILE, COLS),
        buf(TILE, WIDTH),
        buf(4, TILE, COLS),
        buf(2, BLK, COLS),
        buf(2, BLK, COLS),
        buf(TILE, BLK, dtype=F32),
        buf(TILE, COLS),
        pltpu.SemaphoreType.DMA((16,)),
        pltpu.SemaphoreType.DMA((REMOTE,)),
        pltpu.SemaphoreType.DMA((REMOTE,)),
    ]
    return pl.pallas_call(
        kernel,
        out_shape=jax.ShapeDtypeStruct((1024, COLS), BF16),
        in_specs=[any_space, vmem, vmem] + [any_space] * 9 + [smem, smem],
        out_specs=any_space,
        scratch_shapes=scratch,
        compiler_params=pltpu.CompilerParams(
            collective_id=0, has_side_effects=True, vmem_limit_bytes=62 * 2**20
        ),
    )(
        tokens, gain_self, gain_cross, w_query, w_key, w_value,
        w_out.reshape(2, 4, 4, 16, WIDTH), w_cross_query, w_cross_out.reshape(2, 4, 4, 16, WIDTH),
        w_text_key, w_text_value,
        text_states.reshape(2, 4, 128, 1024), song_of_block, last_fill,
    )


def solution(mesh):
    in_specs = (
        P("tm", None),
        P(),
        P(),
        P(None, "mp"),
        P(None, "mp"),
        P(None, "mp"),
        P("mp", None),
        P(None, "mp"),
        P("mp", None),
        P(None, "mp"),
        P(None, "mp"),
        P("tm", None, None),
        P(),
        P(),
    )
    return jax.shard_map(
        on_device, mesh=mesh, in_specs=in_specs, out_specs=P("tm", "mp"), check_vma=False
    )
```
